512 devices in a mesh: row: 16 (over z_hi, x, core), col: 32 (over y, z_lo).
Axes of the slice: x: 4, y: 4, z: 16 (z_hi: 2, z_lo: 8; z = z_hi * 8 + z_lo), core: 2. Of those that a mesh axis runs over, the one named last changes fastest.
Arguments:
- features: bfloat16 [65536, 256], P(('row', 'col')), may hold values from -6 to 6
- order: int32 [512, 128], P(('row', 'col')), may hold values from 0 to 127, each once within a row
- weight: bfloat16 [256, 256], replicated, may hold values from -0.375 to 0.375
- tile_values: bfloat16 [16, 32, 96, 128, 128], P('row', 'col'), may hold values from -0.375 to 0.375
- tile_list: int32 [16, 32, 96, 2], P('row', 'col'), may hold values from -1 to 31, as said below
- cotangent: bfloat16 [65536, 256], P(('row', 'col')), may hold values from -6 to 6
Outputs:
- activated: bfloat16 [65536, 256], P(('row', 'col'))
- feature_grad: bfloat16 [65536, 256], P(('row', 'col'))
- weight_grad: float32 [256, 256], replicated
The draws below stay inside these ranges and needn't reach their ends.
Inputs may be any that keep to these rules, and one draw needn't show every extreme that they name: `tile_list`: on each grid cell the first k slots hold distinct pairs (block row below 32, block column below 16) and the other slots hold -1 in both entries; k is 2 or more everywhere and equals 96 on at least one cell.
All inputs are finite; a program needn't handle non-finite values.
Results may differ from the reference program's by a relative error of at most 0.027.
Values may be sent and summed in bfloat16 or wider, within the bound.
A program may use at most 64 MiB of HBM per device.

```python
import jax
import jax.numpy as jnp
from jax import lax

F = 256
TILE = 128
SLAB = 128
BROWS = 32
BCOLS = 16
TILES_DEV = 96
NODES = 65536
N_ROW = 16
N_COL = 32
DEVICES = 512


def draw_tile_list(key, part):
    key = jax.random.fold_in(key, 7)
    device_count = N_ROW * N_COL
    positions = BROWS * BCOLS
    subkeys = jax.random.split(key, device_count + 2)

    def one_device(subkey):
        return jax.random.permutation(subkey, positions)[:TILES_DEV].astype(jnp.int32)
    chosen = jax.vmap(one_device)(subkeys[:device_count])
    level = jax.random.randint(subkeys[device_count], (device_count,), 1, TILES_DEV + 1)
    occupied = jnp.maximum(level * level // TILES_DEV, 2)
    fullest = jax.random.randint(subkeys[device_count + 1], (), 0, device_count)
    occupied = jnp.where(jnp.arange(device_count) == fullest, TILES_DEV, occupied)
    slot_index = jnp.arange(TILES_DEV)[None, :]
    occupied_slot = slot_index < occupied[:, None]
    block_row = jnp.where(occupied_slot, chosen // BCOLS, -1)
    block_col = jnp.where(occupied_slot, chosen % BCOLS, -1)
    stacked = jnp.stack([block_row, block_col], -1)
    return stacked.reshape(N_ROW, N_COL, TILES_DEV, 2).astype(jnp.int32)


def shard_levels(rng, extent, cuts, least, high):
    def one(position, parts):
        draws = jax.random.uniform(jax.random.fold_in(jax.random.fold_in(rng, 6), position), (parts,), jnp.float32, least / len(cuts), high / len(cuts))
        return jnp.repeat(jnp.exp(draws), extent[position] // parts).reshape((-1,) + (1,) * (len(extent) - position - 1))

    level = one(*cuts[0])
    for cut in cuts[1:]:
        level = level * one(*cut)
    return level


def normal_values(rng, extent, width, reach, shards=(), kind=jnp.bfloat16):
    factor_of = shard_levels(rng, extent, shards, -0.22, 0.18) if shards else 1.0
    values = jax.random.normal(rng, extent, jnp.float32) * width * factor_of
    return jnp.minimum(jnp.maximum(values, -reach), reach).astype(kind)


def setup_inputs(seed: int = 0) -> dict:
    seeds = jax.random.split(jax.random.key(seed), 7)
    return {
        "features": normal_values(seeds[0], (NODES, F), 1.0, 6.0, ((0, 512),)),
        "order": jax.vmap(lambda own: jax.random.permutation(own, SLAB))(jax.random.split(seeds[1], DEVICES)).reshape((DEVICES, SLAB)).astype(jnp.int32),
        "weight": normal_values(seeds[2], (F, F), F ** -0.5, 0.375),
        "tile_values": normal_values(seeds[3], (N_ROW, N_COL, TILES_DEV, TILE, TILE), (2 * TILE) ** -0.5, 0.375, ((0, 16), (1, 32))),
        "tile_list": draw_tile_list(jax.random.fold_in(seeds[6], 71), 0),
        "cotangent": normal_values(seeds[5], (NODES, F), 1.0, 6.0, ((0, 512),)),
    }


def block_products(adjacency_tiles, tile_pairs, source, out_blocks, transpose):
    tile_size = adjacency_tiles.shape[1]
    feature_width = source.shape[1]
    per_round = adjacency_tiles.shape[0] // 6
    occupied = jnp.sum((tile_pairs[:, 0] >= 0).astype(jnp.int32))
    rounds = (occupied + per_round - 1) // per_round
    source_blocks = source.reshape(-1, tile_size, feature_width)
    targets = jnp.arange(out_blocks, dtype=jnp.int32)

    def advance(turn_index, accumulated):
        offset = (turn_index * per_round).astype(jnp.int32)
        tile_piece = lax.dynamic_slice_in_dim(adjacency_tiles, offset, per_round, 0)
        piece_pairs = lax.dynamic_slice_in_dim(tile_pairs, offset, per_round, 0)
        usable = piece_pairs[:, 0] >= 0
        if transpose:
            source_block = jnp.where(usable, piece_pairs[:, 0], 0)
            target_block = piece_pairs[:, 1]
        else:
            source_block = jnp.where(usable, piece_pairs[:, 1], 0)
            target_block = piece_pairs[:, 0]
        picked = jnp.take(source_blocks, source_block, axis=0)
        if transpose:
            products = jnp.einsum("tij,tif->tjf", tile_piece.astype(jnp.float32), picked.astype(jnp.float32))
        else:
            products = jnp.einsum("tij,tjf->tif", tile_piece.astype(jnp.float32), picked.astype(jnp.float32))
        placement = ((target_block[:, None] == targets[None, :]) & usable[:, None]).astype(jnp.float32)
        return accumulated + jnp.einsum("tn,tif->nif", placement, products, precision=lax.Precision.HIGHEST)

    accumulated = lax.fori_loop(0, rounds, advance, jnp.zeros((out_blocks, tile_size, feature_width), jnp.float32))
    return accumulated.reshape(out_blocks * tile_size, feature_width)


def rounded_term(partial_value):
    return lax.optimization_barrier(partial_value.astype(jnp.bfloat16)).astype(jnp.float32)


def reference(features, order, weight, tile_values, tile_list, cotangent):
    slab_count = N_ROW * N_COL
    slab_features = features.reshape(slab_count, SLAB, F)
    clustered = jnp.take_along_axis(slab_features, order[:, :, None], axis=1).reshape(NODES, F)
    projected = jnp.dot(clustered, weight, preferred_element_type=jnp.float32).astype(jnp.bfloat16)
    projected_grid = projected.reshape(N_ROW, N_COL, SLAB, F)
    row_extent = N_COL * SLAB

    def forward_cell(running, device_index):
        row_index = device_index // N_COL
        col_index = device_index % N_COL
        columns = lax.dynamic_index_in_dim(projected_grid, col_index, axis=1, keepdims=False).reshape(N_ROW * SLAB, F)
        partial_value = rounded_term(block_products(tile_values[row_index, col_index], tile_list[row_index, col_index], columns, BROWS, False))
        row_window = lax.dynamic_slice_in_dim(running, row_index * row_extent, row_extent, 0)
        return lax.dynamic_update_slice_in_dim(running, row_window + partial_value, row_index * row_extent, 0), None

    summed, _ = lax.scan(forward_cell, jnp.zeros((NODES, F), jnp.float32), jnp.arange(slab_count, dtype=jnp.int32))
    activated = jax.nn.silu(summed).astype(jnp.bfloat16)
    logistic = jax.nn.sigmoid(summed)
    summed_grad = (cotangent.astype(jnp.float32) * logistic * (1.0 + summed * (1.0 - logistic))).astype(jnp.bfloat16)

    def backward_cell(running, device_index):
        row_index = device_index // N_COL
        col_index = device_index % N_COL
        grad_rows = lax.dynamic_slice_in_dim(summed_grad, row_index * row_extent, row_extent, 0)
        partial_value = rounded_term(block_products(tile_values[row_index, col_index], tile_list[row_index, col_index], grad_rows, BCOLS, True))
        return running.at[:, col_index].add(partial_value.reshape(N_ROW, SLAB, F)), None

    backward_grid, _ = lax.scan(backward_cell, jnp.zeros((N_ROW, N_COL, SLAB, F), jnp.float32), jnp.arange(slab_count, dtype=jnp.int32))
    backward = backward_grid.reshape(NODES, F)
    weight_grad = jnp.dot(clustered.astype(jnp.float32).T, backward, precision=lax.Precision.HIGHEST, preferred_element_type=jnp.float32)
    clustered_grad = jnp.dot(backward, weight.astype(jnp.float32).T, precision=lax.Precision.HIGHEST, preferred_element_type=jnp.float32)
    slab_numbers = jnp.arange(slab_count, dtype=jnp.int32)[:, None]
    feature_grad = jnp.zeros((slab_count, SLAB, F), jnp.float32).at[slab_numbers, order].set(clustered_grad.reshape(slab_count, SLAB, F))
    return activated, feature_grad.reshape(NODES, F).astype(jnp.bfloat16), weight_grad
```

```python
import jax
import jax.numpy as jnp
from jax import lax
from jax.experimental import pallas as pl
from jax.experimental.pallas import tpu as pltpu
from jax.sharding import PartitionSpec as P

MESH = pl.DeviceIdType.MESH
F32 = jnp.float32
BF16 = jnp.bfloat16
VMEM_LIMIT = 48 << 20


def position():
    row, col = lax.axis_index("row"), lax.axis_index("col")
    return row // 8, row // 2 % 4, row % 2, col // 8, col % 8


def device(zh, x, k, y, zl):
    return {"row": zh * 8 + x * 2 + k, "col": y * 8 + zl}


def remote(src, dst, send, recv, target):
    return pltpu.make_async_remote_copy(
        src_ref=src, dst_ref=dst, send_sem=send, recv_sem=recv, device_id=target, device_id_type=MESH
    )


def meet(targets):
    barrier = pltpu.get_barrier_semaphore()
    for target in targets:
        pl.semaphore_signal(barrier, inc=1, device_id=target, device_id_type=MESH)
    pl.semaphore_wait(barrier, len(targets))


def dot(a, b, dims):
    return lax.dot_general(a, b, (dims, ((), ())), preferred_element_type=F32)


def split_dot(a, b, dims):
    high = a.astype(BF16)
    low = (a - high.astype(F32)).astype(BF16)
    return dot(high, b, dims) + dot(low, b, dims)


def chosen(order_ref):
    rows = lax.broadcasted_iota(jnp.int32, (128, 128), 0)
    return jnp.where(rows == order_ref[...], 1.0, 0.0).astype(BF16)


def gather_row_kernel(features, order, blocks, send, recv):
    zh, x, k, y, zl = position()
    sibling = device(zh, x, 1 - k, y, zl)
    other = device(1 - zh, x, k, y, zl)
    beside = [device(zh, (x + d) % 4, k, y, zl) for d in (1, 3, 2)]
    mine = zh * 8 + x * 2 + k
    far = (1 - zh) * 8 + x * 2 + k
    blocks[mine] = dot(chosen(order), features[...], ((0,), (0,))).astype(BF16)
    meet([sibling, other] + beside)
    copies = []

    def push(slot, target):
        copy = remote(blocks.at[slot], blocks.at[slot], send.at[len(copies)], recv.at[slot], target)
        copy.start()
        copies.append(copy)

    def arrived(slot):
        remote(blocks.at[slot], blocks.at[slot], send.at[0], recv.at[slot], sibling).wait_recv()

    push(mine, other)
    for target in beside:
        push(mine, target)
    push(mine, sibling)
    for d in (1, 3, 2):
        slot = zh * 8 + (x + d) % 4 * 2 + k
        arrived(slot)
        push(slot, sibling)
    arrived(far)
    for target in beside:
        push(far, target)
    push(far, sibling)
    for d in (1, 3, 2):
        slot = (1 - zh) * 8 + (x + d) % 4 * 2 + k
        arrived(slot)
        push(slot, sibling)
    for n in range(8):
        arrived(n * 2 + 1 - k)
    for copy in copies:
        copy.wait_send()


def gather_row(features, order):
    return pl.pallas_call(
        gather_row_kernel,
        out_shape=jax.ShapeDtypeStruct((16, 128, 256), BF16),
        in_specs=[pl.BlockSpec(memory_space=pltpu.VMEM)] * 2,
        out_specs=pl.BlockSpec(memory_space=pltpu.VMEM),
        scratch_shapes=[pltpu.SemaphoreType.DMA((16,)), pltpu.SemaphoreType.DMA((16,))],
        compiler_params=pltpu.CompilerParams(collective_id=0, has_side_effects=True, vmem_limit_bytes=VMEM_LIMIT),
        name="gather_row",
    )(features, order)


def products_kernel(transpose, out_blocks, pairs, tiles, source, out, total):
    total[...] = jnp.zeros_like(total)
    unroll = 4

    def step(i, carry):
        picked = []
        for j in range(unroll):
            t = i * unroll + j
            p, q = pairs[2 * t], pairs[2 * t + 1]
            usable = p >= 0
            src, dst = (p, q) if transpose else (q, p)
            src = jnp.where(usable, src, 0)
            dst = jnp.where(usable, dst, out_blocks)
            dims = ((0,), (0,)) if transpose else ((1,), (0,))
            picked.append((dst, dot(tiles[t], source[src], dims)))
        for dst, product in picked:
            total[dst] += product
        return carry

    lax.fori_loop(0, tiles.shape[0] // unroll, step, 0)

    def finish(b, carry):
        out[b] = total[b].astype(BF16)
        return carry

    lax.fori_loop(0, out_blocks, finish, 0)


def products(pairs, tiles, source, out_blocks, transpose):
    def kernel(*refs):
        products_kernel(transpose, out_blocks, *refs)

    return pl.pallas_call(
        kernel,
        out_shape=jax.ShapeDtypeStruct((out_blocks, 128, 256), BF16),
        in_specs=[pl.BlockSpec(memory_space=pltpu.SMEM)] + [pl.BlockSpec(memory_space=pltpu.VMEM)] * 2,
        out_specs=pl.BlockSpec(memory_space=pltpu.VMEM),
        scratch_shapes=[pltpu.VMEM((out_blocks + 1, 128, 256), F32)],
        compiler_params=pltpu.CompilerParams(vmem_limit_bytes=VMEM_LIMIT),
        name="products_back" if transpose else "products",
    )(pairs, tiles, source)


def middle_kernel(
    part, weight, cotangent, activated, grad, piece,
    from_a, from_d, from_s, staged, summed_y, from_z,
    wg, wg_core, wg_y, wg_z, wg_row, wg_sent,
    send_a, send_d, send_s, send_z, recv_a, recv_d, recv_s, recv_z,
    gather_send, gather_recv, wg_send, wg_recv,
):
    zh, x, k, y, zl = position()

    def on_y(d):
        return device(zh, x, k, (y + d + 4) % 4, zl)

    def on_z(z):
        return device(zh, x, k, y, z)

    def block(yy, c):
        return (yy + 4) % 4 * 8 + c

    sibling = device(zh, x, 1 - k, y, zl)
    z_peers = [on_z((zl + d) % 8) for d in range(1, 8)]
    y_peers = [on_y(d) for d in range(1, 4)]
    row_peers = [device((zh + d // 4) % 2, (x + d) % 4, k, y, zl) for d in range(1, 8)]
    meet([sibling] + z_peers + y_peers + row_peers)

    edge = zl + zl // 4 * (7 - 2 * zl)
    inward = 1 - 2 * (zl // 4)

    def ranked(m):
        both = (2 * edge - m + 8) // 8
        alternate = 1 if m % 2 else -1
        way = both * alternate + (1 - both) * inward
        return zl + both * alternate * ((m + 1) // 2) + (1 - both) * inward * (m - edge), way

    order = [ranked(m) for m in range(7, 0, -1)] + [(zl, 0)]
    chunk = [c for c, _ in order]
    turn = [1 - 2 * (c % 2) for c in chunk]
    copies = []

    def go(copy):
        copy.start()
        copies.append(copy)

    def send_antipode(i):
        c = chunk[i]
        go(remote(part.at[block(y + 2, c)], from_a.at[c], send_a.at[c], recv_a.at[c], on_y(turn[i])))

    def send_direct(i):
        c = chunk[i]
        go(remote(part.at[block(y - turn[i], c)], from_d.at[c], send_d.at[c], recv_d.at[c], on_y(-turn[i])))

    def landed(buffer, sem):
        remote(buffer, buffer, sem, sem, sibling).wait_recv()

    def send_sum(i):
        c = chunk[i]
        landed(from_a.at[c], recv_a.at[c])
        staged[c] = (part[block(y + turn[i], c)].astype(F32) + from_a[c].astype(F32)).astype(BF16)
        go(remote(staged.at[c], from_s.at[c], send_s.at[c], recv_s.at[c], on_y(turn[i])))

    def sum_y(i):
        c = chunk[i]
        landed(from_d.at[c], recv_d.at[c])
        landed(from_s.at[c], recv_s.at[c])
        return part[block(y, c)].astype(F32) + from_d[c].astype(F32) + from_s[c].astype(F32)

    def along_z(i):
        c, way = order[i]
        total = sum_y(i)

        @pl.when(edge > 0)
        def _():
            landed(from_z.at[c], recv_z.at[c])
            summed_y[c] = (total + from_z[c].astype(F32)).astype(BF16)

        @pl.when(edge == 0)
        def _():
            summed_y[c] = total.astype(BF16)

        near = (7 - way * (c - zl)) // 6
        slot = c + near * ((1 - way) // 2) * (8 - c)
        go(remote(summed_y.at[c], from_z.at[slot], send_z.at[c], recv_z.at[slot], on_z(zl + way)))

    send_antipode(0)
    send_antipode(1)
    send_direct(0)
    for i in range(8):
        if i + 2 < 8:
            send_antipode(i + 2)
        if i + 1 < 8:
            send_direct(i + 1)
        send_sum(i)
        if i >= 1:
            along_z(i - 1)
    own = sum_y(7)

    @pl.when(zl > 0)
    def _():
        landed(from_z.at[zl], recv_z.at[zl])

    @pl.when(zl < 7)
    def _():
        landed(from_z.at[8], recv_z.at[8])

    left = jnp.where(zl > 0, from_z[zl].astype(F32), 0.0)
    right = jnp.where(zl < 7, from_z[8].astype(F32), 0.0)
    own = own + left + right

    summed = split_dot(own, weight[...], ((1,), (0,)))
    logistic = 1.0 / (1.0 + jnp.exp(-summed))
    gradient = (cotangent[...].astype(F32) * logistic * (1.0 + summed * (1.0 - logistic))).astype(BF16)
    mine = block(y, zl)
    grad[mine] = gradient

    def arrived(slot):
        landed(grad.at[slot], gather_recv.at[slot])

    def pass_on(slot, lane, m, target):
        go(remote(grad.at[slot], grad.at[slot], gather_send.at[lane, m], gather_recv.at[slot], target))

    def conditional(slot, lane, target):
        return remote(grad.at[slot], grad.at[slot], gather_send.at[lane, 0], gather_recv.at[slot], target)

    up = conditional(mine, 0, on_z((zl + 1) % 8))
    down = conditional(mine, 3, on_z((zl + 7) % 8))

    @pl.when(zl < 7)
    def _():
        up.start()

    @pl.when(zl > 0)
    def _():
        down.start()

    pass_on(mine, 1, 0, on_y(1))
    pass_on(mine, 2, 0, on_y(-1))
    activated[...] = (summed * logistic).astype(BF16)
    wg[...] = split_dot_left(own, gradient)
    core_copy = remote(wg.at[pl.ds((1 - k) * 128, 128)], wg_core, wg_send.at[0], wg_recv.at[0], sibling)
    go(core_copy)

    def wg_after_core():
        core_copy.wait_recv()
        wg[pl.ds(pl.multiple_of(k * 128, 128), 128)] += wg_core[...]
        for d in (1, 2, 3):
            rows = pl.ds(pl.multiple_of(k * 128 + (y + d) % 4 * 32, 32), 32)
            go(remote(wg.at[rows], wg_y.at[d], wg_send.at[d], wg_recv.at[d], y_peers[d - 1]))

    def wg_after_y():
        rows = pl.ds(pl.multiple_of(k * 128 + y * 32, 32), 32)
        total = wg[rows]
        for d in (1, 2, 3):
            landed(wg_y.at[d], wg_recv.at[d])
            total = total + wg_y[d]
        for j in range(8):
            wg_sent[j] = total[8 * (j // 2): 8 * (j // 2) + 8, 128 * (j % 2): 128 * (j % 2) + 128]
        for d in range(1, 8):
            go(remote(wg_sent.at[(zl + d) % 8], wg_z.at[d], wg_send.at[3 + d], wg_recv.at[3 + d], z_peers[d - 1]))

    def wg_after_z():
        total = wg_sent[zl]
        for d in range(1, 8):
            landed(wg_z.at[d], wg_recv.at[3 + d])
            total = total + wg_z[d]
        here = zh * 4 + x
        wg_row[here] = total
        for d in range(1, 8):
            go(remote(wg_row.at[here], wg_row.at[here], wg_send.at[10 + d], wg_recv.at[11 + here], row_peers[d - 1]))

    def wg_after_row():
        for d in range(1, 8):
            slot = (zh + d // 4) % 2 * 4 + (x + d) % 4
            landed(wg_row.at[slot], wg_recv.at[11 + slot])
        total = wg_row[0]
        for n in range(1, 8):
            total = total + wg_row[n]
        piece[...] = total

    spread = [(zl, 0)] + [ranked(m) for m in range(1, 8)]
    z_copies = []

    def across(m):
        c = spread[m][0]
        e = 1 - 2 * (c % 2)
        slot = block(y - e, c)
        arrived(slot)
        pass_on(slot, 3 if m else 4, m, on_y(e))

    for m in range(1, 8):
        c, way = spread[m]
        slot = block(y, c)
        arrived(slot)
        forward = remote(
            grad.at[slot], grad.at[slot], gather_send.at[0, m], gather_recv.at[slot], on_z((zl - way + 8) % 8)
        )
        z_copies.append(forward)

        @pl.when(edge > 0)
        def _():
            forward.start()

        pass_on(slot, 1, m, on_y(1))
        pass_on(slot, 2, m, on_y(-1))
        across(m - 1)
        if m == 2:
            wg_after_core()
        if m == 4:
            wg_after_y()
        if m == 6:
            wg_after_z()
    across(7)
    wg_after_row()
    for c in range(8):
        e = 1 - 2 * (c % 2)
        arrived(block(y + e, c))
        arrived(block(y + 2, c))

    @pl.when(zl < 7)
    def _():
        up.wait_send()

    @pl.when(zl > 0)
    def _():
        down.wait_send()

    @pl.when(edge > 0)
    def _():
        for forward in z_copies:
            forward.wait_send()

    for copy in copies:
        copy.wait_send()


def split_dot_left(a, b):
    return split_dot(a, b, ((0,), (0,)))


def middle(part, weight, cotangent):
    slabs = lambda n: pltpu.VMEM((n, 128, 256), BF16)
    dma = pltpu.SemaphoreType.DMA
    return pl.pallas_call(
        middle_kernel,
        out_shape=(
            jax.ShapeDtypeStruct((128, 256), BF16),
            jax.ShapeDtypeStruct((32, 128, 256), BF16),
            jax.ShapeDtypeStruct((8, 128), F32),
        ),
        in_specs=[pl.BlockSpec(memory_space=pltpu.VMEM)] * 3,
        out_specs=(pl.BlockSpec(memory_space=pltpu.VMEM),) * 3,
        scratch_shapes=[
            slabs(8), slabs(8), slabs(8), slabs(8), slabs(8), slabs(9),
            pltpu.VMEM((256, 256), F32), pltpu.VMEM((128, 256), F32), pltpu.VMEM((4, 32, 256), F32),
            pltpu.VMEM((8, 8, 128), F32), pltpu.VMEM((8, 8, 128), F32), pltpu.VMEM((8, 8, 128), F32),
            dma((8,)), dma((8,)), dma((8,)), dma((8,)), dma((8,)), dma((8,)), dma((8,)), dma((9,)),
            dma((5, 8)), dma((32,)), dma((18,)), dma((19,)),
        ],
        compiler_params=pltpu.CompilerParams(collective_id=1, has_side_effects=True, vmem_limit_bytes=VMEM_LIMIT),
        name="middle",
    )(part, weight, cotangent)


def tail_kernel(
    part, weight, order, piece, feature_grad, weight_grad,
    from_core, staged, from_x, own, z_out, from_z, pieces,
    send_core, recv_core, send_x, recv_x, send_z, recv_z, wg_send, wg_z_recv, wg_y_recv, wg_core_recv,
):
    zh, x, k, y, zl = position()
    sibling = device(zh, x, 1 - k, y, zl)
    other = device(1 - zh, x, k, y, zl)
    beside = [device(zh, (x + d) % 4, k, y, zl) for d in range(1, 4)]
    z_peers = [device(zh, x, k, y, (zl + d) % 8) for d in range(1, 8)]
    y_peers = [device(zh, x, k, (y + d) % 4, zl) for d in range(1, 4)]
    pieces[k, y, zl] = piece[...]
    meet([sibling, other] + beside + z_peers + y_peers)
    copies = []

    def go(copy):
        copy.start()
        copies.append(copy)

    def landed(buffer, sem):
        remote(buffer, buffer, sem, sem, sibling).wait_recv()

    turns = [((zh + h) % 2, d) for h in (1, 0) for d in (2, 1, 3, 0)]
    for h, d in turns:
        slot = h * 4 + (x + d) % 4
        go(remote(part.at[slot * 2 + 1 - k], from_core.at[slot], send_core.at[slot], recv_core.at[slot], sibling))
    for d in range(1, 8):
        here = pieces.at[k, y, zl]
        go(remote(here, here, wg_send.at[d], wg_z_recv.at[zl], z_peers[d - 1]))
    for h, d in turns[:4] + turns[4:]:
        slot = h * 4 + (x + d) % 4
        landed(from_core.at[slot], recv_core.at[slot])
        total = part[slot * 2 + k].astype(F32) + from_core[slot].astype(F32)
        if d:
            staged[slot] = total.astype(BF16)
            go(remote(
                staged.at[slot], from_x.at[h * 4 + d], send_x.at[slot], recv_x.at[h * 4 + d], beside[d - 1]
            ))
        else:
            own[h] = total

    for d in range(1, 8):
        landed(pieces.at[k, y, (zl + d) % 8], wg_z_recv.at[(zl + d) % 8])
    for d in range(1, 4):
        here = pieces.at[k, y]
        go(remote(here, here, wg_send.at[7 + d], wg_y_recv.at[y], y_peers[d - 1]))

    def sum_x(h):
        total = own[h]
        for d in range(1, 4):
            landed(from_x.at[h * 4 + d], recv_x.at[h * 4 + d])
            total = total + from_x[h * 4 + d].astype(F32)
        return total

    z_out[...] = sum_x(1 - zh).astype(BF16)
    z_copy = remote(z_out, from_z, send_z, recv_z, other)
    go(z_copy)
    for d in range(1, 4):
        landed(pieces.at[k, (y + d) % 4], wg_y_recv.at[(y + d) % 4])
    core_copy = remote(pieces.at[k], pieces.at[k], wg_send.at[0], wg_core_recv, sibling)
    go(core_copy)
    backward = sum_x(zh)
    landed(pieces.at[1 - k], wg_core_recv)
    for kk in range(2):
        for yy in range(4):
            for j in range(8):
                row = kk * 128 + yy * 32 + j // 2 * 8
                weight_grad[row:row + 8, j % 2 * 128:j % 2 * 128 + 128] = pieces[kk, yy, j]
    z_copy.wait_recv()
    backward = backward + from_z[...].astype(F32)
    clustered_grad = split_dot(backward, weight[...], ((1,), (1,))).astype(BF16)
    feature_grad[...] = dot(chosen(order), clustered_grad, ((1,), (0,))).astype(BF16)
    for copy in copies:
        copy.wait_send()


def tail(part, weight, order, piece):
    dma = pltpu.SemaphoreType.DMA
    slabs = lambda n: pltpu.VMEM((n, 128, 256), BF16)
    return pl.pallas_call(
        tail_kernel,
        out_shape=(jax.ShapeDtypeStruct((128, 256), BF16), jax.ShapeDtypeStruct((256, 256), F32)),
        in_specs=[pl.BlockSpec(memory_space=pltpu.VMEM)] * 4,
        out_specs=(pl.BlockSpec(memory_space=pltpu.VMEM),) * 2,
        scratch_shapes=[
            slabs(8), slabs(8), slabs(8), pltpu.VMEM((2, 128, 256), F32),
            pltpu.VMEM((128, 256), BF16), pltpu.VMEM((128, 256), BF16), pltpu.VMEM((2, 4, 8, 8, 128), F32),
            dma((8,)), dma((8,)), dma((8,)), dma((8,)), dma, dma, dma((11,)), dma((8,)), dma((4,)), dma,
        ],
        compiler_params=pltpu.CompilerParams(collective_id=2, has_side_effects=True, vmem_limit_bytes=VMEM_LIMIT),
        name="tail",
    )(part, weight, order, piece)


def body(features, order, weight, tile_values, tile_list, cotangent):
    tiles = tile_values[0, 0]
    pairs = tile_list[0, 0].reshape(-1)
    columns = gather_row(features, order)
    part = products(pairs, tiles, columns, 32, False)
    activated, grad, piece = middle(part, weight, cotangent)
    back = products(pairs, tiles, grad, 16, True)
    feature_grad, weight_grad = tail(back, weight, order, piece)
    return activated, feature_grad, weight_grad


def solution(mesh):
    placed = (
        P(("row", "col"), None),
        P(("row", "col"), None),
        P(),
        P("row", "col", None, None, None),
        P("row", "col", None, None),
        P(("row", "col"), None),
    )
    return jax.shard_map(
        body,
        mesh=mesh,
        in_specs=placed,
        out_specs=(P(("row", "col"), None), P(("row", "col"), None), P()),
        check_vma=False,
    )
```

```python
import jax
import jax.numpy as jnp
from jax import lax
from jax.experimental import pallas as pl
from jax.experimental.pallas import tpu as pltpu
from jax.sharding import PartitionSpec as P

MESH = pl.DeviceIdType.MESH
F32 = jnp.float32
BF16 = jnp.bfloat16
VMEM_LIMIT = 56 << 20


def position():
    row, col = lax.axis_index("row"), lax.axis_index("col")
    return row // 8, row // 2 % 4, row % 2, col // 8, col % 8


def device(zh, x, k, y, zl):
    return {"row": zh * 8 + x * 2 + k, "col": y * 8 + zl}


def remote(src, dst, send, recv, target):
    return pltpu.make_async_remote_copy(
        src_ref=src, dst_ref=dst, send_sem=send, recv_sem=recv, device_id=target, device_id_type=MESH
    )


def dot(a, b, dims):
    return lax.dot_general(a, b, (dims, ((), ())), preferred_element_type=F32)


def split_dot(a, b, dims):
    high = a.astype(BF16)
    low = (a - high.astype(F32)).astype(BF16)
    return dot(high, b, dims) + dot(low, b, dims)


def chosen(order):
    rows = lax.broadcasted_iota(jnp.int32, (128, 128), 0)
    return jnp.where(rows == order, 1.0, 0.0).astype(BF16)


def tables(pairs, table):
    n = pairs.shape[1]
    down = lax.broadcasted_iota(jnp.int32, (n, n), 0)
    across = lax.broadcasted_iota(jnp.int32, (n, n), 1)
    same = down == across

    def column(row):
        return jnp.sum(jnp.where(same, row, 0), axis=1, keepdims=True)

    p_row, q_row = pairs[0:1, :], pairs[1:2, :]
    lane = lax.broadcasted_iota(jnp.int32, (1, n), 1)
    for base, major_row, minor_row in ((0, p_row, q_row), (4, q_row, p_row)):
        key_row = jnp.where(p_row >= 0, major_row * 32 + minor_row, 2048 + lane)
        key, major, minor = column(key_row), column(major_row), column(minor_row)
        before = key_row < key
        rank = jnp.sum(jnp.where(before, 1, 0), axis=1, keepdims=True)
        goes_on = jnp.sum(jnp.where(before & (major_row == major), 1, 0), axis=1, keepdims=True)
        hit = rank == across

        def sort(values, most):
            return jnp.minimum(jnp.sum(jnp.where(hit, values, 0), axis=0, keepdims=True), most)

        table[base:base + 1, 0:n] = sort(down, n - 1)
        table[base + 1:base + 2, 0:n] = sort(jnp.maximum(minor, 0), 31 if base else 15)
        table[base + 2:base + 3, 0:n] = sort(jnp.minimum(goes_on, 1), 1)
        upto = jnp.sum(jnp.where((major >= 0) & (major <= across), 1, 0), axis=0, keepdims=True)
        here = jnp.sum(jnp.where(major == across, 1, 0), axis=0, keepdims=True)
        table[base + 3:base + 4, 0:n] = jnp.where(here > 0, upto - 1, n)


def layer_kernel(
    features_hbm, order_hbm, weight_hbm, tiles_hbm, pairs_hbm, cotangent_hbm,
    activated, feature_grad, weight_grad,
    features, order, weight, tiles, pairs, cotangent, table, steps, load,
    blocks, prods, part, grad, back,
    from_a, from_d, from_s, staged, summed_y, from_z,
    wg, wg_core, wg_y, wg_z, wg_x, wg_zh, wg_sent, pieces,
    from_core, staged_x, from_x, own_x, zh_out, from_zh,
    row_send, row_recv,
    send_a, send_d, send_s, send_z, recv_a, recv_d, recv_s, recv_z,
    gather_send, gather_recv, wg_send, wg_recv,
    send_core, recv_core, send_x, recv_x, send_zh, recv_zh, back_send, back_recv,
):
    zh, x, k, y, zl = position()

    def on_y(d):
        return device(zh, x, k, (y + d + 4) % 4, zl)

    def on_z(z):
        return device(zh, x, k, y, z)

    def block(yy, c):
        return (yy + 4) % 4 * 8 + c

    sibling = device(zh, x, 1 - k, y, zl)
    other = device(1 - zh, x, k, y, zl)
    x_peers = [device(zh, (x + d) % 4, k, y, zl) for d in (1, 2, 3)]
    y_peers = [on_y(d) for d in (1, 2, 3)]
    z_peers = [on_z((zl + d) % 8) for d in range(1, 8)]
    everyone = [other, sibling] + x_peers + y_peers + z_peers
    barrier = pltpu.get_barrier_semaphore()
    for target in everyone:
        pl.semaphore_signal(barrier, inc=1, device_id=target, device_id_type=MESH)

    loads = [
        pltpu.make_async_copy(hbm, vmem, load.at[n])
        for n, (hbm, vmem) in enumerate((
            (features_hbm, features), (order_hbm, order), (pairs_hbm, pairs),
            (weight_hbm, weight), (cotangent_hbm, cotangent), (tiles_hbm, tiles),
        ))
    ]
    for copy in loads:
        copy.start()
    copies = []

    def go(copy):
        copy.start()
        copies.append(copy)

    def landed(buffer, sem):
        remote(buffer, buffer, sem, sem, sibling).wait_recv()

    mine = zh * 8 + x * 2 + k
    far = (1 - zh) * 8 + x * 2 + k
    loads[0].wait()
    loads[1].wait()
    blocks[mine] = dot(chosen(order[...]), features[...], ((0,), (0,))).astype(BF16)
    loads[2].wait()
    tables(pairs, table)
    to_scalars = pltpu.make_async_copy(table, steps, load.at[6])
    to_scalars.start()
    prods[96] = jnp.zeros((128, 256), BF16)
    pl.semaphore_wait(barrier, len(everyone))
    pushes = [0]

    def push(slot, target):
        go(remote(blocks.at[slot], blocks.at[slot], row_send.at[pushes[0]], row_recv.at[slot], target))
        pushes[0] += 1

    push(mine, other)
    for d in (1, 3, 2):
        push(mine, x_peers[d - 1])
    push(mine, sibling)
    for d in (1, 3, 2):
        slot = zh * 8 + (x + d) % 4 * 2 + k
        landed(blocks.at[slot], row_recv.at[slot])
        push(slot, sibling)
    landed(blocks.at[far], row_recv.at[far])
    for d in (1, 3, 2):
        push(far, x_peers[d - 1])
    push(far, sibling)
    for d in (1, 3, 2):
        slot = (1 - zh) * 8 + (x + d) % 4 * 2 + k
        landed(blocks.at[slot], row_recv.at[slot])
        push(slot, sibling)
    for copy in loads[3:]:
        copy.wait()
    to_scalars.wait()
    for n in range(8):
        slot = n * 2 + 1 - k
        landed(blocks.at[slot], row_recv.at[slot])

    def products(source, base, dims, out):
        unroll = 4

        def step(i, total):
            for j in range(unroll):
                s = i * unroll + j
                product = dot(tiles[steps[base, s]], source[steps[base + 1, s]], dims)
                total = total * steps[base + 2, s].astype(F32) + product
                prods[s] = total.astype(BF16)
            return total

        lax.fori_loop(0, 96 // unroll, step, jnp.zeros((128, 256), F32))

        def pick(b, carry):
            out[b] = prods[steps[base + 3, b]]
            return carry

        lax.fori_loop(0, out.shape[0], pick, 0)

    products(blocks, 0, ((1,), (0,)), part)

    near, half = zl % 4, zl // 4
    partner = on_z((zl + 4) % 8)
    edge = near + near // 2 * (3 - 2 * near)
    inward = 1 - 2 * (near // 2)

    def ranked(m):
        both = (2 * edge - m + 4) // 4
        alternate = 1 if m % 2 else -1
        return near + both * alternate * ((m + 1) // 2) + (1 - both) * inward * (m - edge)

    nearest = [ranked(m) for m in (1, 2, 3)]

    place = [nearest[2], nearest[1], nearest[0], near] * 2
    chunk = [(1 - half) * 4 + n for n in place[:4]] + [half * 4 + n for n in place[4:]]
    turn = [1 - 2 * (n % 2) for n in place]
    def send_antipode(i):
        c = chunk[i]
        go(remote(part.at[block(y + 2, c)], from_a.at[c], send_a.at[c], recv_a.at[c], on_y(turn[i])))

    def send_direct(i):
        c = chunk[i]
        go(remote(part.at[block(y - turn[i], c)], from_d.at[c], send_d.at[c], recv_d.at[c], on_y(-turn[i])))

    def send_sum(i):
        c = chunk[i]
        landed(from_a.at[c], recv_a.at[c])
        staged[c] = (part[block(y + turn[i], c)].astype(F32) + from_a[c].astype(F32)).astype(BF16)
        go(remote(staged.at[c], from_s.at[c], send_s.at[c], recv_s.at[c], on_y(turn[i])))

    def sum_y(i):
        c = chunk[i]
        landed(from_d.at[c], recv_d.at[c])
        landed(from_s.at[c], recv_s.at[c])
        return part[block(y, c)].astype(F32) + from_d[c].astype(F32) + from_s[c].astype(F32)

    def to_place(i):
        c = chunk[i]
        summed_y[c] = sum_y(i).astype(BF16)
        slot = i // 4 * 4 + near
        go(remote(summed_y.at[c], from_z.at[slot], send_z.at[c], recv_z.at[slot], on_z(half * 4 + place[i])))

    def sum_half(i):
        total = sum_y(i)
        for d in (1, 2, 3):
            slot = i // 4 * 4 + (near + d) % 4
            landed(from_z.at[slot], recv_z.at[slot])
            total = total + from_z[slot].astype(F32)
        return total

    send_antipode(0)
    send_antipode(1)
    send_direct(0)
    for i in range(8):
        if i + 2 < 8:
            send_antipode(i + 2)
        if i + 1 < 8:
            send_direct(i + 1)
        send_sum(i)
        if 1 <= i <= 3 or 5 <= i:
            to_place(i - 1)
        if i == 5:
            c = chunk[3]
            summed_y[c] = sum_half(3).astype(BF16)
            go(remote(summed_y.at[c], from_z.at[8], send_z.at[c], recv_z.at[8], partner))
    own = sum_half(7)
    landed(from_z.at[8], recv_z.at[8])
    own = own + from_z[8].astype(F32)

    summed = split_dot(own, weight[...], ((1,), (0,)))
    logistic = 1.0 / (1.0 + jnp.exp(-summed))
    gradient = (cotangent[...].astype(F32) * logistic * (1.0 + summed * (1.0 - logistic))).astype(BF16)
    here = block(y, zl)
    grad[here] = gradient

    def arrived(slot):
        landed(grad.at[slot], gather_recv.at[slot])

    def pass_on(slot, lane, m, target):
        go(remote(grad.at[slot], grad.at[slot], gather_send.at[lane, m], gather_recv.at[slot], target))

    def to_half(slot, lane):
        for m in range(3):
            pass_on(slot, lane, m, on_z(half * 4 + nearest[m]))

    pass_on(here, 3, 3, partner)
    to_half(here, 3)
    pass_on(here, 1, 0, on_y(1))
    pass_on(here, 2, 0, on_y(-1))
    activated[...] = (summed * logistic).astype(BF16)
    wg[...] = split_dot(own, gradient, ((0,), (0,)))
    core_copy = remote(wg.at[pl.ds((1 - k) * 128, 128)], wg_core, wg_send.at[0], wg_recv.at[0], sibling)
    go(core_copy)

    def wg_after_core():
        core_copy.wait_recv()
        wg[pl.ds(pl.multiple_of(k * 128, 128), 128)] += wg_core[...]
        for d in (1, 2, 3):
            rows = pl.ds(pl.multiple_of(k * 128 + (y + d) % 4 * 32, 32), 32)
            go(remote(wg.at[rows], wg_y.at[d], wg_send.at[d], wg_recv.at[d], y_peers[d - 1]))

    def wg_after_y():
        rows = pl.ds(pl.multiple_of(k * 128 + y * 32, 32), 32)
        total = wg[rows]
        for d in (1, 2, 3):
            landed(wg_y.at[d], wg_recv.at[d])
            total = total + wg_y[d]
        for j in range(8):
            wg_sent[j] = total[8 * (j // 2): 8 * (j // 2) + 8, 128 * (j % 2): 128 * (j % 2) + 128]
        for d in range(1, 8):
            go(remote(wg_sent.at[(zl + d) % 8], wg_z.at[d], wg_send.at[3 + d], wg_recv.at[3 + d], z_peers[d - 1]))

    def wg_after_z():
        total = wg_sent[zl]
        for d in range(1, 8):
            landed(wg_z.at[d], wg_recv.at[3 + d])
            total = total + wg_z[d]
        wg_x[x] = total
        for d in (1, 2, 3):
            go(remote(wg_x.at[x], wg_x.at[x], wg_send.at[10 + d], wg_recv.at[11 + x], x_peers[d - 1]))

    def wg_after_x():
        for d in (1, 2, 3):
            landed(wg_x.at[(x + d) % 4], wg_recv.at[11 + (x + d) % 4])
        wg_zh[zh] = wg_x[0] + wg_x[1] + wg_x[2] + wg_x[3]
        go(remote(wg_zh.at[zh], wg_zh.at[zh], wg_send.at[14], wg_recv.at[15 + zh], other))

    def wg_after_zh():
        landed(wg_zh.at[1 - zh], wg_recv.at[16 - zh])
        mine_at = pieces.at[k, y, zl]
        pieces[k, y, zl] = wg_zh[0] + wg_zh[1]
        for d in range(1, 8):
            go(remote(mine_at, mine_at, back_send.at[d], back_recv.at[zl], z_peers[d - 1]))

    def wg_back_y():
        for d in range(1, 8):
            landed(pieces.at[k, y, (zl + d) % 8], back_recv.at[(zl + d) % 8])
        for d in (1, 2, 3):
            go(remote(pieces.at[k, y], pieces.at[k, y], back_send.at[7 + d], back_recv.at[8 + y], y_peers[d - 1]))

    def wg_back_core():
        for d in (1, 2, 3):
            landed(pieces.at[k, (y + d) % 4], back_recv.at[8 + (y + d) % 4])
        go(remote(pieces.at[k], pieces.at[k], back_send.at[0], back_recv.at[12], sibling))

    def wg_finish():
        landed(pieces.at[1 - k], back_recv.at[12])
        for kk in range(2):
            for yy in range(4):
                for j in range(8):
                    row = kk * 128 + yy * 32 + j // 2 * 8
                    weight_grad[row:row + 8, j % 2 * 128:j % 2 * 128 + 128] = pieces[kk, yy, j]

    spread = [zl] + [half * 4 + n for n in nearest] + [(zl + 4) % 8] + [(1 - half) * 4 + n for n in nearest]

    def across(m):
        c = spread[m]
        e = 1 - 2 * (c % 2)
        slot = block(y - e, c)
        arrived(slot)
        pass_on(slot, 0, m, on_y(e))

    for m in range(1, 8):
        slot = block(y, spread[m])
        arrived(slot)
        if m == 4:
            to_half(slot, 4)
        pass_on(slot, 1, m, on_y(1))
        pass_on(slot, 2, m, on_y(-1))
        across(m - 1)
        if m == 2:
            wg_after_core()
        if m == 4:
            wg_after_y()
    across(7)
    wg_after_z()
    for c in range(8):
        e = 1 - 2 * (c % 2)
        arrived(block(y + e, c))
        arrived(block(y + 2, c))
    wg_after_x()

    products(grad, 4, ((0,), (0,)), back)

    for h, d in [(1 - zh, d) for d in (2, 1, 3, 0)] + [(zh, d) for d in (2, 1, 3, 0)]:
        slot = h * 4 + (x + d) % 4
        go(remote(back.at[slot * 2 + 1 - k], from_core.at[slot], send_core.at[slot], recv_core.at[slot], sibling))

    def to_x(h):
        for d in (2, 1, 3, 0):
            slot = h * 4 + (x + d) % 4
            landed(from_core.at[slot], recv_core.at[slot])
            total = back[slot * 2 + k].astype(F32) + from_core[slot].astype(F32)
            if d:
                staged_x[slot] = total.astype(BF16)
                go(remote(
                    staged_x.at[slot], from_x.at[h * 4 + d], send_x.at[slot], recv_x.at[h * 4 + d], x_peers[d - 1]
                ))
            else:
                own_x[h] = total

    def sum_x(h):
        total = own_x[h]
        for d in (1, 2, 3):
            landed(from_x.at[h * 4 + d], recv_x.at[h * 4 + d])
            total = total + from_x[h * 4 + d].astype(F32)
        return total

    to_x(1 - zh)
    wg_after_zh()
    to_x(zh)
    zh_out[...] = sum_x(1 - zh).astype(BF16)
    go(remote(zh_out, from_zh, send_zh, recv_zh, other))
    wg_back_y()
    backward = sum_x(zh)
    wg_back_core()
    wg_finish()
    landed(from_zh, recv_zh)
    backward = backward + from_zh[...].astype(F32)
    clustered_grad = split_dot(backward, weight[...], ((1,), (1,))).astype(BF16)
    feature_grad[...] = dot(chosen(order[...]), clustered_grad, ((1,), (0,))).astype(BF16)
    for copy in copies:
        copy.wait_send()


def body(features, order, weight, tile_values, tile_list, cotangent):
    dma = pltpu.SemaphoreType.DMA

    def slabs(n):
        return pltpu.VMEM((n, 128, 256), BF16)

    return pl.pallas_call(
        layer_kernel,
        out_shape=(
            jax.ShapeDtypeStruct((128, 256), BF16),
            jax.ShapeDtypeStruct((128, 256), BF16),
            jax.ShapeDtypeStruct((256, 256), F32),
        ),
        in_specs=[pl.BlockSpec(memory_space=pl.ANY)] * 6,
        out_specs=(pl.BlockSpec(memory_space=pltpu.VMEM),) * 3,
        scratch_shapes=[
            pltpu.VMEM((128, 256), BF16), pltpu.VMEM((1, 128), jnp.int32), pltpu.VMEM((256, 256), BF16),
            pltpu.VMEM((96, 128, 128), BF16), pltpu.VMEM((2, 96), jnp.int32), pltpu.VMEM((128, 256), BF16),
            pltpu.VMEM((8, 128), jnp.int32), pltpu.SMEM((8, 128), jnp.int32), dma((7,)),
            slabs(16), slabs(97), slabs(32), slabs(32), slabs(16),
            slabs(8), slabs(8), slabs(8), slabs(8), slabs(8), slabs(9),
            pltpu.VMEM((256, 256), F32), pltpu.VMEM((128, 256), F32), pltpu.VMEM((4, 32, 256), F32),
            pltpu.VMEM((8, 8, 128), F32), pltpu.VMEM((4, 8, 128), F32), pltpu.VMEM((2, 8, 128), F32),
            pltpu.VMEM((8, 8, 128), F32), pltpu.VMEM((2, 4, 8, 8, 128), F32),
            slabs(8), slabs(8), slabs(8), pltpu.VMEM((2, 128, 256), F32),
            pltpu.VMEM((128, 256), BF16), pltpu.VMEM((128, 256), BF16),
            dma((16,)), dma((16,)),
            dma((8,)), dma((8,)), dma((8,)), dma((8,)), dma((8,)), dma((8,)), dma((8,)), dma((9,)),
            dma((5, 8)), dma((32,)), dma((15,)), dma((17,)),
            dma((8,)), dma((8,)), dma((8,)), dma((8,)), dma, dma, dma((11,)), dma((13,)),
        ],
        compiler_params=pltpu.CompilerParams(collective_id=0, has_side_effects=True, vmem_limit_bytes=VMEM_LIMIT),
        name="layer",
    )(features, order, weight, tile_values[0, 0], tile_list[0, 0].T, cotangent)


def solution(mesh):
    placed = (
        P(("row", "col"), None),
        P(("row", "col"), None),
        P(),
        P("row", "col", None, None, None),
        P("row", "col", None, None),
        P(("row", "col"), None),
    )
    return jax.shard_map(
        body,
        mesh=mesh,
        in_specs=placed,
        out_specs=(P(("row", "col"), None), P(("row", "col"), None), P()),
        check_vma=False,
    )
```

```python
import jax
import jax.numpy as jnp
from jax import lax
from jax.experimental import pallas as pl
from jax.experimental.pallas import tpu as pltpu
from jax.sharding import PartitionSpec as P

MESH = pl.DeviceIdType.MESH
F32 = jnp.float32
BF16 = jnp.bfloat16
VMEM_LIMIT = 52 << 20


def position():
    row, col = lax.axis_index("row"), lax.axis_index("col")
    return row // 8, row // 2 % 4, row % 2, col // 8, col % 8


def device(zh, x, k, y, zl):
    return {"row": zh * 8 + x * 2 + k, "col": y * 8 + zl}


def remote(src, dst, send, recv, target):
    return pltpu.make_async_remote_copy(
        src_ref=src, dst_ref=dst, send_sem=send, recv_sem=recv, device_id=target, device_id_type=MESH
    )


def dot(a, b, dims):
    return lax.dot_general(a, b, (dims, ((), ())), preferred_element_type=F32)


def split_dot(a, b, dims):
    high = a.astype(BF16)
    low = (a - high.astype(F32)).astype(BF16)
    return dot(high, b, dims) + dot(low, b, dims)


def chosen(order):
    rows = lax.broadcasted_iota(jnp.int32, (128, 128), 0)
    return jnp.where(rows == order, 1.0, 0.0).astype(BF16)


def tables(pairs, table):
    n = pairs.shape[1]
    down = lax.broadcasted_iota(jnp.int32, (n, n), 0)
    across = lax.broadcasted_iota(jnp.int32, (n, n), 1)
    same = down == across

    def column(row):
        return jnp.sum(jnp.where(same, row, 0), axis=1, keepdims=True)

    p_row, q_row = pairs[0:1, :], pairs[1:2, :]
    lane = lax.broadcasted_iota(jnp.int32, (1, n), 1)
    for base, major_row, minor_row in ((0, p_row, q_row), (4, q_row, p_row)):
        key_row = jnp.where(p_row >= 0, major_row * 32 + minor_row, 2048 + lane)
        key, major, minor = column(key_row), column(major_row), column(minor_row)
        before = key_row < key
        rank = jnp.sum(jnp.where(before, 1, 0), axis=1, keepdims=True)
        goes_on = jnp.sum(jnp.where(before & (major_row == major), 1, 0), axis=1, keepdims=True)
        hit = rank == across

        def sort(values, most):
            return jnp.minimum(jnp.sum(jnp.where(hit, values, 0), axis=0, keepdims=True), most)

        table[base:base + 1, 0:n] = sort(down, n - 1)
        table[base + 1:base + 2, 0:n] = sort(jnp.maximum(minor, 0), 31 if base else 15)
        table[base + 2:base + 3, 0:n] = sort(jnp.minimum(goes_on, 1), 1)
        upto = jnp.sum(jnp.where((major >= 0) & (major <= across), 1, 0), axis=0, keepdims=True)
        here = jnp.sum(jnp.where(major == across, 1, 0), axis=0, keepdims=True)
        table[base + 3:base + 4, 0:n] = jnp.where(here > 0, upto - 1, n)


def layer_kernel(
    features_hbm, order_hbm, weight_hbm, tiles_hbm, pairs_hbm, cotangent_hbm,
    activated, feature_grad, weight_grad,
    features, order, weight, tiles, pairs, cotangent, table, steps, load,
    blocks, prods, part, grad, back,
    from_a, from_d, from_s, staged, summed_y, from_z,
    wg, wg_core, wg_x, wg_y, wg_z,
    from_core, staged_x, from_x, own_x, zh_out, from_zh,
    row_send, row_recv,
    send_a, send_d, send_s, send_z, recv_a, recv_d, recv_s, recv_z,
    gather_send, gather_recv, wg_send, wg_recv,
    send_core, recv_core, send_x, recv_x, send_zh, recv_zh, back_send, back_recv,
):
    zh, x, k, y, zl = position()

    def on_y(d):
        return device(zh, x, k, (y + d + 4) % 4, zl)

    def on_z(z):
        return device(zh, x, k, y, z)

    def block(yy, c):
        return (yy + 4) % 4 * 8 + c

    sibling = device(zh, x, 1 - k, y, zl)
    other = device(1 - zh, x, k, y, zl)
    x_peers = [device(zh, (x + d) % 4, k, y, zl) for d in (1, 2, 3)]
    y_peers = [on_y(d) for d in (1, 2, 3)]
    z = zh * 8 + zl
    z_peers = [device((z + d) % 16 // 8, x, k, y, (z + d) % 8) for d in range(1, 16)]
    everyone = [sibling] + x_peers + y_peers + z_peers
    barrier = pltpu.get_barrier_semaphore()
    for target in everyone:
        pl.semaphore_signal(barrier, inc=1, device_id=target, device_id_type=MESH)

    loads = [
        pltpu.make_async_copy(hbm, vmem, load.at[n])
        for n, (hbm, vmem) in enumerate((
            (features_hbm, features), (order_hbm, order), (pairs_hbm, pairs),
            (weight_hbm, weight), (cotangent_hbm, cotangent), (tiles_hbm, tiles),
        ))
    ]
    for copy in loads:
        copy.start()
    copies = []

    def go(copy):
        copy.start()
        copies.append(copy)

    def landed(buffer, sem):
        remote(buffer, buffer, sem, sem, sibling).wait_recv()

    mine = zh * 8 + x * 2 + k
    far = (1 - zh) * 8 + x * 2 + k
    loads[0].wait()
    loads[1].wait()
    blocks[mine] = dot(chosen(order[...]), features[...], ((0,), (0,))).astype(BF16)
    loads[2].wait()
    tables(pairs, table)
    to_scalars = pltpu.make_async_copy(table, steps, load.at[6])
    to_scalars.start()
    prods[96] = jnp.zeros((128, 256), BF16)
    pl.semaphore_wait(barrier, len(everyone))
    pushes = [0]

    def cut_block(slot, part_of):
        return blocks.at[slot] if part_of is None else blocks.at[slot, pl.ds(part_of * 64, 64)]

    def push(slot, target, part_of=None):
        view = cut_block(slot, part_of)
        go(remote(view, view, row_send.at[pushes[0]], row_recv.at[slot, part_of or 0], target))
        pushes[0] += 1

    def got(slot, part_of=None):
        landed(cut_block(slot, part_of), row_recv.at[slot, part_of or 0])

    push(mine, other, 0)
    push(mine, other, 1)
    for d in (2, 1, 3):
        push(mine, x_peers[d - 1])
    push(mine, sibling)
    for d in (1, 3, 2):
        slot = zh * 8 + (x + d) % 4 * 2 + k
        got(slot)
        push(slot, sibling)
    for part_of in (0, 1):
        got(far, part_of)
        for d in (2, 1, 3):
            push(far, x_peers[d - 1], part_of)
        push(far, sibling, part_of)
    for part_of in (0, 1):
        for d in (1, 3, 2):
            slot = (1 - zh) * 8 + (x + d) % 4 * 2 + k
            got(slot, part_of)
            push(slot, sibling, part_of)
    for copy in loads[3:]:
        copy.wait()
    to_scalars.wait()
    for n in range(4):
        got(zh * 8 + n * 2 + 1 - k)
        got((1 - zh) * 8 + n * 2 + 1 - k, 0)
        got((1 - zh) * 8 + n * 2 + 1 - k, 1)

    def products(source, base, dims, out):
        unroll = 4

        def step(i, total):
            for j in range(unroll):
                s = i * unroll + j
                product = dot(tiles[steps[base, s]], source[steps[base + 1, s]], dims)
                total = total * steps[base + 2, s].astype(F32) + product
                prods[s] = total.astype(BF16)
            return total

        lax.fori_loop(0, 96 // unroll, step, jnp.zeros((128, 256), F32))

        def pick(b, carry):
            out[b] = prods[steps[base + 3, b]]
            return carry

        lax.fori_loop(0, out.shape[0], pick, 0)

    products(blocks, 0, ((1,), (0,)), part)

    near, half = zl % 4, zl // 4
    partner = on_z((zl + 4) % 8)
    edge = near + near // 2 * (3 - 2 * near)
    inward = 1 - 2 * (near // 2)

    def ranked(m):
        both = (2 * edge - m + 4) // 4
        alternate = 1 if m % 2 else -1
        return near + both * alternate * ((m + 1) // 2) + (1 - both) * inward * (m - edge)

    nearest = [ranked(m) for m in (1, 2, 3)]

    place = [nearest[2], nearest[1], nearest[0], near]
    units = [((1 - half) * 4 + n, n, rows, 64) for rows in (0, 64) for n in place]
    units += [(half * 4 + n, n, 0, 128) for n in place]

    def cut(buffer, index, u):
        return buffer.at[index, pl.ds(units[u][2], units[u][3])]

    def read(buffer, index, u):
        return buffer[index, pl.ds(units[u][2], units[u][3])].astype(F32)

    def sem(group, u):
        return group.at[units[u][0], units[u][2] // 64]

    def turn(u):
        return 1 - 2 * (units[u][1] % 2)

    def send_antipode(u):
        c = units[u][0]
        go(remote(cut(part, block(y + 2, c), u), cut(from_a, c, u), sem(send_a, u), sem(recv_a, u), on_y(turn(u))))

    def send_direct(u):
        c = units[u][0]
        source = cut(part, block(y - turn(u), c), u)
        go(remote(source, cut(from_d, c, u), sem(send_d, u), sem(recv_d, u), on_y(-turn(u))))

    def send_sum(u):
        c, _, rows, count = units[u]
        landed(cut(from_a, c, u), sem(recv_a, u))
        total = read(part, block(y + turn(u), c), u) + read(from_a, c, u)
        staged[c, pl.ds(rows, count)] = total.astype(BF16)
        go(remote(cut(staged, c, u), cut(from_s, c, u), sem(send_s, u), sem(recv_s, u), on_y(turn(u))))

    def sum_y(u):
        c = units[u][0]
        landed(cut(from_d, c, u), sem(recv_d, u))
        landed(cut(from_s, c, u), sem(recv_s, u))
        return read(part, block(y, c), u) + read(from_d, c, u) + read(from_s, c, u)

    def to_place(u):
        c, n, rows, count = units[u]
        summed_y[c, pl.ds(rows, count)] = sum_y(u).astype(BF16)
        slot = u // 8 * 4 + near
        arrival = recv_z.at[slot, rows // 64]
        go(remote(cut(summed_y, c, u), cut(from_z, slot, u), sem(send_z, u), arrival, on_z(half * 4 + n)))

    def sum_half(u):
        total = sum_y(u)
        for d in (1, 2, 3):
            slot = u // 8 * 4 + (near + d) % 4
            landed(cut(from_z, slot, u), recv_z.at[slot, units[u][2] // 64])
            total = total + read(from_z, slot, u)
        return total

    def to_partner(u):
        c, _, rows, count = units[u]
        summed_y[c, pl.ds(rows, count)] = sum_half(u).astype(BF16)
        arrival = recv_z.at[8, rows // 64]
        go(remote(cut(summed_y, c, u), cut(from_z, 8, u), sem(send_z, u), arrival, partner))

    def run(action, *numbers):
        for u in numbers:
            action(u)

    run(send_antipode, *range(8))
    run(send_direct, 0, 1)
    run(send_sum, 0, 1)
    run(send_direct, 2, 3)
    run(send_sum, 2, 3)
    run(send_direct, 4, 5)
    run(send_sum, 4, 5)
    run(send_direct, 6, 7)
    run(send_sum, 6, 7)
    run(send_antipode, 8, 9, 10, 11)
    run(to_place, 0, 1, 2)
    run(send_direct, 8, 9)
    run(to_place, 4, 5, 6)
    run(to_partner, 3)
    run(send_sum, 8, 9)
    run(send_direct, 10, 11)
    run(send_sum, 10, 11)
    run(to_partner, 7)
    run(to_place, 8, 9, 10)
    own = sum_half(11)
    landed(from_z.at[8, pl.ds(0, 64)], recv_z.at[8, 0])
    landed(from_z.at[8, pl.ds(64, 64)], recv_z.at[8, 1])
    own = own + from_z[8].astype(F32)

    summed = split_dot(own, weight[...], ((1,), (0,)))
    logistic = 1.0 / (1.0 + jnp.exp(-summed))
    gradient = (cotangent[...].astype(F32) * logistic * (1.0 + summed * (1.0 - logistic))).astype(BF16)
    here = block(y, zl)
    grad[here] = gradient

    def cut_grad(slot, part_of):
        return grad.at[slot] if part_of is None else grad.at[slot, pl.ds(part_of * 64, 64)]

    def arrived(slot, part_of=None):
        landed(cut_grad(slot, part_of), gather_recv.at[slot, part_of or 0])

    sent = [0]

    def pass_on(slot, part_of, target):
        view = cut_grad(slot, part_of)
        go(remote(view, view, gather_send.at[sent[0]], gather_recv.at[slot, part_of or 0], target))
        sent[0] += 1

    def to_half(slot, part_of):
        for n in nearest:
            pass_on(slot, part_of, on_z(half * 4 + n))

    def to_sides(slot, part_of=None):
        pass_on(slot, part_of, on_y(1))
        pass_on(slot, part_of, on_y(-1))

    def across(c, part_of=None):
        e = 1 - 2 * (c % 2)
        slot = block(y - e, c)
        arrived(slot, part_of)
        pass_on(slot, part_of, on_y(e))

    pass_on(here, 0, partner)
    pass_on(here, 1, partner)
    to_sides(here)
    to_half(here, None)
    activated[...] = (summed * logistic).astype(BF16)
    wg[...] = split_dot(own, gradient, ((0,), (0,)))
    core_copy = remote(wg.at[pl.ds((1 - k) * 128, 128)], wg_core, wg_send.at[0], wg_recv.at[0], sibling)
    go(core_copy)

    def wg_after_core():
        core_copy.wait_recv()
        wg[pl.ds(pl.multiple_of(k * 128, 128), 128)] += wg_core[...]
        for d in (1, 2, 3):
            rows = pl.ds(pl.multiple_of(k * 128 + (x + d) % 4 * 32, 32), 32)
            go(remote(wg.at[rows], wg_x.at[d], wg_send.at[d], wg_recv.at[d], x_peers[d - 1]))

    def wg_after_x():
        rows = pl.ds(pl.multiple_of(k * 128 + x * 32, 32), 32)
        for d in (1, 2, 3):
            landed(wg_x.at[d], wg_recv.at[d])
        wg_x[0] = wg[rows] + wg_x[1] + wg_x[2] + wg_x[3]
        for d in (1, 2, 3):
            rows = pl.ds(pl.multiple_of((y + d) % 4 * 8, 8), 8)
            go(remote(wg_x.at[0, rows], wg_y.at[d], wg_send.at[3 + d], wg_recv.at[3 + d], y_peers[d - 1]))

    def wg_after_y():
        total = wg_x[0, pl.ds(pl.multiple_of(y * 8, 8), 8)]
        for d in (1, 2, 3):
            landed(wg_y.at[d], wg_recv.at[3 + d])
            total = total + wg_y[d]
        wg_z[z] = total
        for d in range(1, 16):
            go(remote(wg_z.at[z], wg_z.at[z], wg_send.at[6 + d], wg_recv.at[7 + z], z_peers[d - 1]))

    def wg_rows(kk, xx, yy, count):
        return weight_grad.at[pl.ds(pl.multiple_of(kk * 128 + xx * 32 + yy * 8, 8), count)]

    def wg_after_z():
        for d in range(1, 16):
            landed(wg_z.at[(z + d) % 16], wg_recv.at[7 + (z + d) % 16])
        total = wg_z[0]
        for n in range(1, 16):
            total = total + wg_z[n]
        mine_at = wg_rows(k, x, y, 8)
        mine_at[...] = total
        for d in (1, 2, 3):
            go(remote(mine_at, mine_at, back_send.at[d], back_recv.at[y], y_peers[d - 1]))

    def wg_back_x():
        for d in (1, 2, 3):
            landed(wg_rows(k, x, (y + d) % 4, 8), back_recv.at[(y + d) % 4])
        mine_at = wg_rows(k, x, 0, 32)
        for d in (1, 2, 3):
            go(remote(mine_at, mine_at, back_send.at[3 + d], back_recv.at[4 + x], x_peers[d - 1]))

    def wg_back_core():
        for d in (1, 2, 3):
            landed(wg_rows(k, (x + d) % 4, 0, 32), back_recv.at[4 + (x + d) % 4])
        mine_at = wg_rows(k, 0, 0, 128)
        go(remote(mine_at, mine_at, back_send.at[0], back_recv.at[8], sibling))

    def wg_finish():
        landed(wg_rows(1 - k, 0, 0, 128), back_recv.at[8])

    close = [half * 4 + n for n in nearest]
    beyond = (zl + 4) % 8
    distant = [(1 - half) * 4 + n for n in nearest]

    def take(c, part_of=None):
        slot = block(y, c)
        arrived(slot, part_of)
        if c is beyond:
            to_half(slot, part_of)
        to_sides(slot, part_of)

    for c in close:
        take(c)
    across(zl)
    wg_after_core()
    take(beyond, 0)
    across(close[0])
    take(beyond, 1)
    across(close[1])
    across(close[2])
    wg_after_x()
    for c in distant:
        take(c, 0)
    across(beyond, 0)
    for c in distant:
        take(c, 1)
    across(beyond, 1)
    for c in distant:
        across(c, 0)
    wg_after_y()
    for c in distant:
        across(c, 1)
    for c in [zl] + close:
        e = 1 - 2 * (c % 2)
        arrived(block(y + e, c))
        arrived(block(y + 2, c))
    for c in [beyond] + distant:
        e = 1 - 2 * (c % 2)
        for part_of in (0, 1):
            arrived(block(y + e, c), part_of)
            arrived(block(y + 2, c), part_of)
    products(grad, 4, ((0,), (0,)), back)

    for h, d in [(1 - zh, d) for d in (2, 1, 3, 0)] + [(zh, d) for d in (2, 1, 3, 0)]:
        slot = h * 4 + (x + d) % 4
        go(remote(back.at[slot * 2 + 1 - k], from_core.at[slot], send_core.at[slot], recv_core.at[slot], sibling))

    def exchanged(h):
        for d in (2, 1, 3, 0):
            slot = h * 4 + (x + d) % 4
            landed(from_core.at[slot], recv_core.at[slot])

    def to_x(h, rows, count):
        some = pl.ds(rows, count)
        for d in (2, 1, 3, 0):
            slot = h * 4 + (x + d) % 4
            total = back[slot * 2 + k, some].astype(F32) + from_core[slot, some].astype(F32)
            if d:
                staged_x[slot, some] = total.astype(BF16)
                go(remote(
                    staged_x.at[slot, some], from_x.at[h * 4 + d, some], send_x.at[slot, rows // 64],
                    recv_x.at[h * 4 + d, rows // 64], x_peers[d - 1]
                ))
            else:
                own_x[h, some] = total

    def sum_x(h, rows, count):
        some = pl.ds(rows, count)
        total = own_x[h, some]
        for d in (1, 3, 2):
            landed(from_x.at[h * 4 + d, some], recv_x.at[h * 4 + d, rows // 64])
            total = total + from_x[h * 4 + d, some].astype(F32)
        return total

    wg_after_z()
    exchanged(1 - zh)
    to_x(1 - zh, 0, 64)
    to_x(1 - zh, 64, 64)
    exchanged(zh)
    to_x(zh, 0, 128)
    for n in (0, 1):
        some = pl.ds(n * 64, 64)
        zh_out[some] = sum_x(1 - zh, n * 64, 64).astype(BF16)
        go(remote(zh_out.at[some], from_zh.at[some], send_zh.at[n], recv_zh.at[n], other))
    wg_back_x()
    backward = sum_x(zh, 0, 128)
    wg_back_core()
    wg_finish()
    for n in (0, 1):
        landed(from_zh.at[pl.ds(n * 64, 64)], recv_zh.at[n])
    backward = backward + from_zh[...].astype(F32)
    clustered_grad = split_dot(backward, weight[...], ((1,), (1,))).astype(BF16)
    feature_grad[...] = dot(chosen(order[...]), clustered_grad, ((1,), (0,))).astype(BF16)
    for copy in copies:
        copy.wait_send()


def body(features, order, weight, tile_values, tile_list, cotangent):
    dma = pltpu.SemaphoreType.DMA

    def slabs(n):
        return pltpu.VMEM((n, 128, 256), BF16)

    return pl.pallas_call(
        layer_kernel,
        out_shape=(
            jax.ShapeDtypeStruct((128, 256), BF16),
            jax.ShapeDtypeStruct((128, 256), BF16),
            jax.ShapeDtypeStruct((256, 256), F32),
        ),
        in_specs=[pl.BlockSpec(memory_space=pltpu.HBM)] * 6,
        out_specs=(pl.BlockSpec(memory_space=pltpu.VMEM),) * 3,
        scratch_shapes=[
            pltpu.VMEM((128, 256), BF16), pltpu.VMEM((1, 128), jnp.int32), pltpu.VMEM((256, 256), BF16),
            pltpu.VMEM((96, 128, 128), BF16), pltpu.VMEM((2, 96), jnp.int32), pltpu.VMEM((128, 256), BF16),
            pltpu.VMEM((8, 128), jnp.int32), pltpu.SMEM((8, 128), jnp.int32), dma((7,)),
            slabs(16), slabs(97), slabs(32), slabs(32), slabs(16),
            slabs(8), slabs(8), slabs(8), slabs(8), slabs(8), slabs(9),
            pltpu.VMEM((256, 256), F32), pltpu.VMEM((128, 256), F32), pltpu.VMEM((4, 32, 256), F32),
            pltpu.VMEM((4, 8, 256), F32), pltpu.VMEM((16, 8, 256), F32),
            slabs(8), slabs(8), slabs(8), pltpu.VMEM((2, 128, 256), F32),
            pltpu.VMEM((128, 256), BF16), pltpu.VMEM((128, 256), BF16),
            dma((23,)), dma((16, 2)),
            dma((8, 2)), dma((8, 2)), dma((8, 2)), dma((8, 2)), dma((8, 2)), dma((8, 2)), dma((8, 2)), dma((9, 2)),
            dma((53,)), dma((32, 2)), dma((22,)), dma((23,)),
            dma((8,)), dma((8,)), dma((8, 2)), dma((8, 2)), dma((2,)), dma((2,)), dma((7,)), dma((9,)),
        ],
        compiler_params=pltpu.CompilerParams(collective_id=0, has_side_effects=True, vmem_limit_bytes=VMEM_LIMIT),
        name="layer",
    )(features, order, weight, tile_values[0, 0], tile_list[0, 0].T, cotangent)


def solution(mesh):
    placed = (
        P(("row", "col"), None),
        P(("row", "col"), None),
        P(),
        P("row", "col", None, None, None),
        P("row", "col", None, None),
        P(("row", "col"), None),
    )
    return jax.shard_map(
        body,
        mesh=mesh,
        in_specs=placed,
        out_specs=(P(("row", "col"), None), P(("row", "col"), None), P()),
        check_vma=False,
    )
```

```python
import jax
import jax.numpy as jnp
from jax import lax
from jax.experimental import pallas as pl
from jax.experimental.pallas import tpu as pltpu
from jax.sharding import PartitionSpec as P

MESH = pl.DeviceIdType.MESH
F32 = jnp.float32
BF16 = jnp.bfloat16
VMEM_LIMIT = 52 << 20


def position():
    row, col = lax.axis_index("row"), lax.axis_index("col")
    return row // 8, row // 2 % 4, row % 2, col // 8, col % 8


def device(zh, x, k, y, zl):
    return {"row": zh * 8 + x * 2 + k, "col": y * 8 + zl}


def remote(src, dst, send, recv, target):
    return pltpu.make_async_remote_copy(
        src_ref=src, dst_ref=dst, send_sem=send, recv_sem=recv, device_id=target, device_id_type=MESH
    )


def dot(a, b, dims):
    return lax.dot_general(a, b, (dims, ((), ())), preferred_element_type=F32)


def split_dot(a, b, dims):
    high = a.astype(BF16)
    low = (a - high.astype(F32)).astype(BF16)
    return dot(high, b, dims) + dot(low, b, dims)


def chosen(order):
    rows = lax.broadcasted_iota(jnp.int32, (128, 128), 0)
    return jnp.where(rows == order, 1.0, 0.0).astype(BF16)


def tables(pairs, table):
    n = pairs.shape[1]
    down = lax.broadcasted_iota(jnp.int32, (n, n), 0)
    across = lax.broadcasted_iota(jnp.int32, (n, n), 1)
    same = down == across

    def column(row):
        return jnp.sum(jnp.where(same, row, 0), axis=1, keepdims=True)

    p_row, q_row = pairs[0:1, :], pairs[1:2, :]
    lane = lax.broadcasted_iota(jnp.int32, (1, n), 1)
    for base, major_row, minor_row in ((0, p_row, q_row), (4, q_row, p_row)):
        key_row = jnp.where(p_row >= 0, major_row * 32 + minor_row, 2048 + lane)
        key, major, minor = column(key_row), column(major_row), column(minor_row)
        before = key_row < key
        rank = jnp.sum(jnp.where(before, 1, 0), axis=1, keepdims=True)
        goes_on = jnp.sum(jnp.where(before & (major_row == major), 1, 0), axis=1, keepdims=True)
        hit = rank == across

        def sort(values, most):
            return jnp.minimum(jnp.sum(jnp.where(hit, values, 0), axis=0, keepdims=True), most)

        table[base:base + 1, 0:n] = sort(down, n - 1)
        table[base + 1:base + 2, 0:n] = sort(jnp.maximum(minor, 0), 31 if base else 15)
        table[base + 2:base + 3, 0:n] = sort(jnp.minimum(goes_on, 1), 1)
        upto = jnp.sum(jnp.where((major >= 0) & (major <= across), 1, 0), axis=0, keepdims=True)
        here = jnp.sum(jnp.where(major == across, 1, 0), axis=0, keepdims=True)
        table[base + 3:base + 4, 0:n] = jnp.where(here > 0, upto - 1, n)


def layer_kernel(
    features_hbm, order_hbm, weight_hbm, tiles_hbm, pairs_hbm, cotangent_hbm,
    activated, feature_grad, weight_grad,
    features, order, weight, tiles, pairs, cotangent, table, steps, load,
    blocks, prods, part, grad, back,
    from_a, from_d, from_s, staged, summed_y, from_z,
    wg, wg_core, wg_x, wg_y, wg_z,
    from_core, staged_x, from_x, own_x, zh_out, from_zh,
    row_send, row_recv,
    send_a, send_d, send_s, send_z, recv_a, recv_d, recv_s, recv_z,
    gather_send, gather_recv, wg_send, wg_recv,
    send_core, recv_core, send_x, recv_x, send_zh, recv_zh, back_send, back_recv,
):
    zh, x, k, y, zl = position()

    def on_y(d):
        return device(zh, x, k, (y + d + 4) % 4, zl)

    def on_z(z):
        return device(zh, x, k, y, z)

    def block(yy, c):
        return (yy + 4) % 4 * 8 + c

    sibling = device(zh, x, 1 - k, y, zl)
    other = device(1 - zh, x, k, y, zl)
    x_peers = [device(zh, (x + d) % 4, k, y, zl) for d in (1, 2, 3)]
    y_peers = [on_y(d) for d in (1, 2, 3)]
    z = zh * 8 + zl
    z_peers = [device((z + d) % 16 // 8, x, k, y, (z + d) % 8) for d in range(1, 16)]
    everyone = [sibling] + x_peers + y_peers + z_peers
    barrier = pltpu.get_barrier_semaphore()
    for target in everyone:
        pl.semaphore_signal(barrier, inc=1, device_id=target, device_id_type=MESH)

    loads = [
        pltpu.make_async_copy(hbm, vmem, load.at[n])
        for n, (hbm, vmem) in enumerate((
            (features_hbm, features), (order_hbm, order), (pairs_hbm, pairs),
            (weight_hbm, weight), (cotangent_hbm, cotangent), (tiles_hbm, tiles),
        ))
    ]
    for copy in loads:
        copy.start()
    copies = []

    def go(copy):
        copy.start()
        copies.append(copy)

    def landed(buffer, sem):
        remote(buffer, buffer, sem, sem, sibling).wait_recv()

    mine = zh * 8 + x * 2 + k
    far = (1 - zh) * 8 + x * 2 + k
    loads[0].wait()
    loads[1].wait()
    blocks[mine] = dot(chosen(order[...]), features[...], ((0,), (0,))).astype(BF16)
    loads[2].wait()
    tables(pairs, table)
    to_scalars = pltpu.make_async_copy(table, steps, load.at[6])
    to_scalars.start()
    prods[96] = jnp.zeros((128, 256), BF16)
    pl.semaphore_wait(barrier, len(everyone))
    pushes = [0]

    def cut_block(slot, part_of):
        return blocks.at[slot] if part_of is None else blocks.at[slot, pl.ds(part_of * 64, 64)]

    def push(slot, target, part_of=None):
        view = cut_block(slot, part_of)
        go(remote(view, view, row_send.at[pushes[0]], row_recv.at[slot, part_of or 0], target))
        pushes[0] += 1

    def got(slot, part_of=None):
        landed(cut_block(slot, part_of), row_recv.at[slot, part_of or 0])

    push(mine, other, 0)
    push(mine, other, 1)
    for d in (2, 1, 3):
        push(mine, x_peers[d - 1])
    push(mine, sibling)
    for d in (1, 3, 2):
        slot = zh * 8 + (x + d) % 4 * 2 + k
        got(slot)
        push(slot, sibling)
    for part_of in (0, 1):
        got(far, part_of)
        for d in (2, 1, 3):
            push(far, x_peers[d - 1], part_of)
        push(far, sibling, part_of)
    for part_of in (0, 1):
        for d in (1, 3, 2):
            slot = (1 - zh) * 8 + (x + d) % 4 * 2 + k
            got(slot, part_of)
            push(slot, sibling, part_of)
    for copy in loads[3:]:
        copy.wait()
    to_scalars.wait()
    for n in range(4):
        got(zh * 8 + n * 2 + 1 - k)
        got((1 - zh) * 8 + n * 2 + 1 - k, 0)
        got((1 - zh) * 8 + n * 2 + 1 - k, 1)

    def products(source, base, dims):
        unroll = 32

        def step(i, total):
            for j in range(unroll):
                s = i * unroll + j
                product = dot(tiles[steps[base, s]], source[steps[base + 1, s]], dims)
                total = total * steps[base + 2, s].astype(F32) + product
                prods[s] = total.astype(BF16)
            return total

        lax.fori_loop(0, 96 // unroll, step, jnp.zeros((128, 256), F32))

    def pick(out, b, base):
        out[b] = prods[steps[base + 3, b]]

    products(blocks, 0, ((1,), (0,)))

    near, half = zl % 4, zl // 4
    partner = on_z((zl + 4) % 8)
    edge = near + near // 2 * (3 - 2 * near)
    inward = 1 - 2 * (near // 2)

    def ranked(m):
        both = (2 * edge - m + 4) // 4
        alternate = 1 if m % 2 else -1
        return near + both * alternate * ((m + 1) // 2) + (1 - both) * inward * (m - edge)

    nearest = [ranked(m) for m in (1, 2, 3)]

    place = [nearest[2], nearest[1], nearest[0], near]
    units = [((1 - half) * 4 + n, n, rows, 64) for rows in (0, 64) for n in place]
    units += [(half * 4 + n, n, 0, 128) for n in place]

    def cut(buffer, index, u):
        return buffer.at[index, pl.ds(units[u][2], units[u][3])]

    def read(buffer, index, u):
        return buffer[index, pl.ds(units[u][2], units[u][3])].astype(F32)

    def sem(group, u):
        return group.at[units[u][0], units[u][2] // 64]

    def turn(u):
        return 1 - 2 * (units[u][1] % 2)

    def send_antipode(u):
        c = units[u][0]
        go(remote(cut(part, block(y + 2, c), u), cut(from_a, c, u), sem(send_a, u), sem(recv_a, u), on_y(turn(u))))

    def send_direct(u):
        c = units[u][0]
        source = cut(part, block(y - turn(u), c), u)
        go(remote(source, cut(from_d, c, u), sem(send_d, u), sem(recv_d, u), on_y(-turn(u))))

    def send_sum(u):
        c, _, rows, count = units[u]
        landed(cut(from_a, c, u), sem(recv_a, u))
        total = read(part, block(y + turn(u), c), u) + read(from_a, c, u)
        staged[c, pl.ds(rows, count)] = total.astype(BF16)
        go(remote(cut(staged, c, u), cut(from_s, c, u), sem(send_s, u), sem(recv_s, u), on_y(turn(u))))

    def sum_y(u):
        c = units[u][0]
        landed(cut(from_d, c, u), sem(recv_d, u))
        landed(cut(from_s, c, u), sem(recv_s, u))
        return read(part, block(y, c), u) + read(from_d, c, u) + read(from_s, c, u)

    def to_place(u):
        c, n, rows, count = units[u]
        summed_y[c, pl.ds(rows, count)] = sum_y(u).astype(BF16)
        slot = u // 8 * 4 + near
        arrival = recv_z.at[slot, rows // 64]
        go(remote(cut(summed_y, c, u), cut(from_z, slot, u), sem(send_z, u), arrival, on_z(half * 4 + n)))

    def sum_half(u):
        total = sum_y(u)
        for d in (1, 2, 3):
            slot = u // 8 * 4 + (near + d) % 4
            landed(cut(from_z, slot, u), recv_z.at[slot, units[u][2] // 64])
            total = total + read(from_z, slot, u)
        return total

    def to_partner(u):
        c, _, rows, count = units[u]
        summed_y[c, pl.ds(rows, count)] = sum_half(u).astype(BF16)
        arrival = recv_z.at[8, rows // 64]
        go(remote(cut(summed_y, c, u), cut(from_z, 8, u), sem(send_z, u), arrival, partner))

    def run(action, *numbers):
        for u in numbers:
            action(u)

    for i in range(4):
        pick(part, block(y + 2, units[i][0]), 0)
        send_antipode(i)
    run(send_antipode, 4, 5, 6, 7)
    for i in range(4):
        pick(part, block(y - turn(i), units[i][0]), 0)
        send_direct(i)
    for i in range(4):
        pick(part, block(y + turn(i), units[i][0]), 0)
        pick(part, block(y, units[i][0]), 0)
    run(send_sum, 0, 1)
    run(send_direct, 4, 5)
    run(send_sum, 2, 3)
    run(send_direct, 6, 7)
    run(send_sum, 4, 5, 6, 7)
    for i in range(8, 12):
        pick(part, block(y + 2, units[i][0]), 0)
        send_antipode(i)
    for i in range(8, 12):
        for d in (1, 3, 0):
            pick(part, block(y + d, units[i][0]), 0)
    run(to_place, 0, 1, 2)
    run(send_direct, 8, 9)
    run(to_place, 4, 5, 6)
    run(to_partner, 3)
    run(send_sum, 8, 9)
    run(send_direct, 10, 11)
    run(send_sum, 10, 11)
    run(to_partner, 7)
    run(to_place, 8, 9, 10)
    own = sum_half(11)
    landed(from_z.at[8, pl.ds(0, 64)], recv_z.at[8, 0])
    landed(from_z.at[8, pl.ds(64, 64)], recv_z.at[8, 1])
    own = own + from_z[8].astype(F32)

    summed = split_dot(own, weight[...], ((1,), (0,)))
    logistic = 1.0 / (1.0 + jnp.exp(-summed))
    gradient = (cotangent[...].astype(F32) * logistic * (1.0 + summed * (1.0 - logistic))).astype(BF16)
    here = block(y, zl)
    grad[here] = gradient

    def cut_grad(slot, part_of):
        return grad.at[slot] if part_of is None else grad.at[slot, pl.ds(part_of * 64, 64)]

    def arrived(slot, part_of=None):
        landed(cut_grad(slot, part_of), gather_recv.at[slot, part_of or 0])

    sent = [0]

    def pass_on(slot, part_of, target):
        view = cut_grad(slot, part_of)
        go(remote(view, view, gather_send.at[sent[0]], gather_recv.at[slot, part_of or 0], target))
        sent[0] += 1

    def to_half(slot, part_of):
        for n in nearest:
            pass_on(slot, part_of, on_z(half * 4 + n))

    def to_sides(slot, part_of=None):
        pass_on(slot, part_of, on_y(1))
        pass_on(slot, part_of, on_y(-1))

    def across(c, part_of=None):
        e = 1 - 2 * (c % 2)
        slot = block(y - e, c)
        arrived(slot, part_of)
        pass_on(slot, part_of, on_y(e))

    pass_on(here, 0, partner)
    pass_on(here, 1, partner)
    to_sides(here)
    to_half(here, None)
    activated[...] = (summed * logistic).astype(BF16)
    wg[...] = split_dot(own, gradient, ((0,), (0,)))
    core_copy = remote(wg.at[pl.ds((1 - k) * 128, 128)], wg_core, wg_send.at[0], wg_recv.at[0], sibling)
    go(core_copy)

    def wg_after_core():
        core_copy.wait_recv()
        wg[pl.ds(pl.multiple_of(k * 128, 128), 128)] += wg_core[...]
        for d in (1, 2, 3):
            rows = pl.ds(pl.multiple_of(k * 128 + (x + d) % 4 * 32, 32), 32)
            go(remote(wg.at[rows], wg_x.at[d], wg_send.at[d], wg_recv.at[d], x_peers[d - 1]))

    def wg_after_x():
        rows = pl.ds(pl.multiple_of(k * 128 + x * 32, 32), 32)
        for d in (1, 2, 3):
            landed(wg_x.at[d], wg_recv.at[d])
        wg_x[0] = wg[rows] + wg_x[1] + wg_x[2] + wg_x[3]
        for d in (1, 2, 3):
            rows = pl.ds(pl.multiple_of((y + d) % 4 * 8, 8), 8)
            go(remote(wg_x.at[0, rows], wg_y.at[d], wg_send.at[3 + d], wg_recv.at[3 + d], y_peers[d - 1]))

    def wg_after_y():
        total = wg_x[0, pl.ds(pl.multiple_of(y * 8, 8), 8)]
        for d in (1, 2, 3):
            landed(wg_y.at[d], wg_recv.at[3 + d])
            total = total + wg_y[d]
        wg_z[z] = total
        for d in range(1, 16):
            go(remote(wg_z.at[z], wg_z.at[z], wg_send.at[6 + d], wg_recv.at[7 + z], z_peers[d - 1]))

    def wg_rows(kk, xx, yy, count):
        return weight_grad.at[pl.ds(pl.multiple_of(kk * 128 + xx * 32 + yy * 8, 8), count)]

    def wg_after_z():
        for d in range(1, 16):
            landed(wg_z.at[(z + d) % 16], wg_recv.at[7 + (z + d) % 16])
        total = wg_z[0]
        for n in range(1, 16):
            total = total + wg_z[n]
        mine_at = wg_rows(k, x, y, 8)
        mine_at[...] = total
        for d in (1, 2, 3):
            go(remote(mine_at, mine_at, back_send.at[d], back_recv.at[y], y_peers[d - 1]))

    def wg_back_x():
        for d in (1, 2, 3):
            landed(wg_rows(k, x, (y + d) % 4, 8), back_recv.at[(y + d) % 4])
        mine_at = wg_rows(k, x, 0, 32)
        for d in (1, 2, 3):
            go(remote(mine_at, mine_at, back_send.at[3 + d], back_recv.at[4 + x], x_peers[d - 1]))

    def wg_back_core():
        for d in (1, 2, 3):
            landed(wg_rows(k, (x + d) % 4, 0, 32), back_recv.at[4 + (x + d) % 4])
        mine_at = wg_rows(k, 0, 0, 128)
        go(remote(mine_at, mine_at, back_send.at[0], back_recv.at[8], sibling))

    def wg_finish():
        landed(wg_rows(1 - k, 0, 0, 128), back_recv.at[8])

    close = [half * 4 + n for n in nearest]
    beyond = (zl + 4) % 8
    distant = [(1 - half) * 4 + n for n in nearest]

    def take(c, part_of=None):
        slot = block(y, c)
        arrived(slot, part_of)
        if c is beyond:
            to_half(slot, part_of)
        to_sides(slot, part_of)

    for c in close:
        take(c)
    across(zl)
    wg_after_core()
    take(beyond, 0)
    across(close[0])
    take(beyond, 1)
    across(close[1])
    across(close[2])
    wg_after_x()
    for c in distant:
        take(c, 0)
    across(beyond, 0)
    for c in distant:
        take(c, 1)
    across(beyond, 1)
    for c in distant:
        across(c, 0)
    wg_after_y()
    for c in distant:
        across(c, 1)
    for c in [zl] + close:
        e = 1 - 2 * (c % 2)
        arrived(block(y + e, c))
        arrived(block(y + 2, c))
    for c in [beyond] + distant:
        e = 1 - 2 * (c % 2)
        for part_of in (0, 1):
            arrived(block(y + e, c), part_of)
            arrived(block(y + 2, c), part_of)
    products(grad, 4, ((0,), (0,)))

    turns = [(h, d) for h in (1 - zh, zh) for d in (2, 1, 3, 0)]
    for h, d in turns:
        slot = h * 4 + (x + d) % 4
        pick(back, slot * 2 + 1 - k, 4)
        go(remote(back.at[slot * 2 + 1 - k], from_core.at[slot], send_core.at[slot], recv_core.at[slot], sibling))
    for h, d in turns:
        pick(back, (h * 4 + (x + d) % 4) * 2 + k, 4)

    def exchanged(h):
        for d in (2, 1, 3, 0):
            slot = h * 4 + (x + d) % 4
            landed(from_core.at[slot], recv_core.at[slot])

    def to_x(h, rows, count):
        some = pl.ds(rows, count)
        for d in (2, 1, 3, 0):
            slot = h * 4 + (x + d) % 4
            total = back[slot * 2 + k, some].astype(F32) + from_core[slot, some].astype(F32)
            if d:
                staged_x[slot, some] = total.astype(BF16)
                go(remote(
                    staged_x.at[slot, some], from_x.at[h * 4 + d, some], send_x.at[slot, rows // 64],
                    recv_x.at[h * 4 + d, rows // 64], x_peers[d - 1]
                ))
            else:
                own_x[h, some] = total

    def sum_x(h, rows, count):
        some = pl.ds(rows, count)
        total = own_x[h, some]
        for d in (1, 3, 2):
            landed(from_x.at[h * 4 + d, some], recv_x.at[h * 4 + d, rows // 64])
            total = total + from_x[h * 4 + d, some].astype(F32)
        return total

    exchanged(1 - zh)
    to_x(1 - zh, 0, 64)
    to_x(1 - zh, 64, 64)
    exchanged(zh)
    to_x(zh, 0, 128)
    wg_after_z()
    for n in (0, 1):
        some = pl.ds(n * 64, 64)
        zh_out[some] = sum_x(1 - zh, n * 64, 64).astype(BF16)
        go(remote(zh_out.at[some], from_zh.at[some], send_zh.at[n], recv_zh.at[n], other))
    wg_back_x()
    backward = sum_x(zh, 0, 128)
    wg_back_core()
    for copy in copies:
        copy.wait_send()
    wg_finish()
    placed = chosen(order[...])
    total = jnp.zeros((128, 256), F32)
    for n in (0, 1):
        landed(from_zh.at[pl.ds(n * 64, 64)], recv_zh.at[n])
        rows = backward[n * 64:n * 64 + 64] + from_zh[n * 64:n * 64 + 64].astype(F32)
        clustered_grad = split_dot(rows, weight[...], ((1,), (1,))).astype(BF16)
        total = total + dot(placed[:, n * 64:n * 64 + 64], clustered_grad, ((1,), (0,)))
    feature_grad[...] = total.astype(BF16)


def body(features, order, weight, tile_values, tile_list, cotangent):
    dma = pltpu.SemaphoreType.DMA

    def slabs(n):
        return pltpu.VMEM((n, 128, 256), BF16)

    operands = (features, order, weight, tile_values[0, 0], tile_list[0, 0].T, cotangent)
    return pl.pallas_call(
        layer_kernel,
        out_shape=(
            jax.ShapeDtypeStruct((128, 256), BF16),
            jax.ShapeDtypeStruct((128, 256), BF16),
            jax.ShapeDtypeStruct((256, 256), F32),
        ),
        in_specs=[pl.BlockSpec(memory_space=pltpu.HBM)] * 6,
        out_specs=(pl.BlockSpec(memory_space=pltpu.VMEM),) * 3,
        scratch_shapes=[
            pltpu.VMEM((128, 256), BF16), pltpu.VMEM((1, 128), jnp.int32), pltpu.VMEM((256, 256), BF16),
            pltpu.VMEM((96, 128, 128), BF16), pltpu.VMEM((2, 96), jnp.int32), pltpu.VMEM((128, 256), BF16),
            pltpu.VMEM((8, 128), jnp.int32), pltpu.SMEM((8, 128), jnp.int32), dma((7,)),
            slabs(16), slabs(97), slabs(32), slabs(32), slabs(16),
            slabs(8), slabs(8), slabs(8), slabs(8), slabs(8), slabs(9),
            pltpu.VMEM((256, 256), F32), pltpu.VMEM((128, 256), F32), pltpu.VMEM((4, 32, 256), F32),
            pltpu.VMEM((4, 8, 256), F32), pltpu.VMEM((16, 8, 256), F32),
            slabs(8), slabs(8), slabs(8), pltpu.VMEM((2, 128, 256), F32),
            pltpu.VMEM((128, 256), BF16), pltpu.VMEM((128, 256), BF16),
            dma((23,)), dma((16, 2)),
            dma((8, 2)), dma((8, 2)), dma((8, 2)), dma((8, 2)), dma((8, 2)), dma((8, 2)), dma((8, 2)), dma((9, 2)),
            dma((53,)), dma((32, 2)), dma((22,)), dma((23,)),
            dma((8,)), dma((8,)), dma((8, 2)), dma((8, 2)), dma((2,)), dma((2,)), dma((7,)), dma((9,)),
        ],
        compiler_params=pltpu.CompilerParams(collective_id=0, has_side_effects=True, vmem_limit_bytes=VMEM_LIMIT),
        name="layer",
    )(*[pltpu.with_memory_space_constraint(operand, pltpu.HBM) for operand in operands])


def solution(mesh):
    placed = (
        P(("row", "col"), None),
        P(("row", "col"), None),
        P(),
        P("row", "col", None, None, None),
        P("row", "col", None, None),
        P(("row", "col"), None),
    )
    return jax.shard_map(
        body,
        mesh=mesh,
        in_specs=placed,
        out_specs=(P(("row", "col"), None), P(("row", "col"), None), P()),
        check_vma=False,
    )
```

```python
import jax
import jax.numpy as jnp
from jax import lax
from jax.experimental import pallas as pl
from jax.experimental.pallas import tpu as pltpu
from jax.sharding import PartitionSpec as P

MESH = pl.DeviceIdType.MESH
F32 = jnp.float32
BF16 = jnp.bfloat16
VMEM_LIMIT = 52 << 20


def position():
    row, col = lax.axis_index("row"), lax.axis_index("col")
    return row // 8, row // 2 % 4, row % 2, col // 8, col % 8


def device(zh, x, k, y, zl):
    return {"row": zh * 8 + x * 2 + k, "col": y * 8 + zl}


def remote(src, dst, send, recv, target):
    return pltpu.make_async_remote_copy(
        src_ref=src, dst_ref=dst, send_sem=send, recv_sem=recv, device_id=target, device_id_type=MESH
    )


def dot(a, b, dims):
    return lax.dot_general(a, b, (dims, ((), ())), preferred_element_type=F32)


def split_dot(a, b, dims):
    high = a.astype(BF16)
    low = (a - high.astype(F32)).astype(BF16)
    return dot(high, b, dims) + dot(low, b, dims)


def chosen(order):
    rows = lax.broadcasted_iota(jnp.int32, (128, 128), 0)
    return jnp.where(rows == order, 1.0, 0.0).astype(BF16)


def tables(pairs, table):
    n = pairs.shape[1]
    down = lax.broadcasted_iota(jnp.int32, (n, n), 0)
    across = lax.broadcasted_iota(jnp.int32, (n, n), 1)
    same = down == across

    def column(row):
        return jnp.sum(jnp.where(same, row, 0), axis=1, keepdims=True)

    p_row, q_row = pairs[0:1, :], pairs[1:2, :]
    lane = lax.broadcasted_iota(jnp.int32, (1, n), 1)
    for base, major_row, minor_row in ((0, p_row, q_row), (4, q_row, p_row)):
        key_row = jnp.where(p_row >= 0, major_row * 32 + minor_row, 2048 + lane)
        key, major, minor = column(key_row), column(major_row), column(minor_row)
        before = key_row < key
        rank = jnp.sum(jnp.where(before, 1, 0), axis=1, keepdims=True)
        goes_on = jnp.sum(jnp.where(before & (major_row == major), 1, 0), axis=1, keepdims=True)
        hit = rank == across

        def sort(values, most):
            return jnp.minimum(jnp.sum(jnp.where(hit, values, 0), axis=0, keepdims=True), most)

        table[base:base + 1, 0:n] = sort(down, n - 1)
        table[base + 1:base + 2, 0:n] = sort(jnp.maximum(minor, 0), 31 if base else 15)
        table[base + 2:base + 3, 0:n] = sort(jnp.minimum(goes_on, 1), 1)
        upto = jnp.sum(jnp.where((major >= 0) & (major <= across), 1, 0), axis=0, keepdims=True)
        here = jnp.sum(jnp.where(major == across, 1, 0), axis=0, keepdims=True)
        table[base + 3:base + 4, 0:n] = jnp.where(here > 0, upto - 1, n)


def layer_kernel(
    features_hbm, order_hbm, weight_hbm, tiles_hbm, pairs_hbm, cotangent_hbm,
    activated, feature_grad, weight_grad,
    features, order, weight, tiles, pairs, cotangent, table, steps, load,
    blocks, prods, part, grad, back,
    from_a, from_d, from_s, staged, summed_y, from_z,
    wg, wg_core, wg_x, wg_y, wg_z,
    from_core, staged_x, from_x, own_x, zh_out, from_zh,
    row_send, row_recv,
    send_a, send_d, send_s, send_z, recv_a, recv_d, recv_s, recv_z,
    gather_send, gather_recv, wg_send, wg_recv,
    send_core, recv_core, send_x, recv_x, send_zh, recv_zh, back_send, back_recv,
):
    zh, x, k, y, zl = position()

    def on_y(d):
        return device(zh, x, k, (y + d + 4) % 4, zl)

    def on_z(z):
        return device(zh, x, k, y, z)

    def block(yy, c):
        return (yy + 4) % 4 * 8 + c

    sibling = device(zh, x, 1 - k, y, zl)
    other = device(1 - zh, x, k, y, zl)
    x_peers = [device(zh, (x + d) % 4, k, y, zl) for d in (1, 2, 3)]
    y_peers = [on_y(d) for d in (1, 2, 3)]
    z = zh * 8 + zl
    z_peers = [device((z + d) % 16 // 8, x, k, y, (z + d) % 8) for d in range(1, 16)]
    everyone = [sibling] + x_peers + y_peers + z_peers
    barrier = pltpu.get_barrier_semaphore()
    for target in everyone:
        pl.semaphore_signal(barrier, inc=1, device_id=target, device_id_type=MESH)

    loads = [
        pltpu.make_async_copy(hbm, vmem, load.at[n])
        for n, (hbm, vmem) in enumerate((
            (features_hbm, features), (order_hbm, order), (pairs_hbm, pairs),
            (weight_hbm, weight), (cotangent_hbm, cotangent), (tiles_hbm, tiles),
        ))
    ]
    for copy in loads:
        copy.start()
    copies = []

    def go(copy):
        copy.start()
        copies.append(copy)

    def landed(buffer, sem):
        remote(buffer, buffer, sem, sem, sibling).wait_recv()

    mine = zh * 8 + x * 2 + k
    far = (1 - zh) * 8 + x * 2 + k
    loads[0].wait()
    loads[1].wait()
    blocks[mine] = dot(chosen(order[...]), features[...], ((0,), (0,))).astype(BF16)
    loads[2].wait()
    pl.semaphore_wait(barrier, len(everyone))
    pushes = [0]

    def cut_block(slot, part_of):
        return blocks.at[slot] if part_of is None else blocks.at[slot, pl.ds(part_of * 64, 64)]

    def push(slot, target, part_of=None):
        view = cut_block(slot, part_of)
        go(remote(view, view, row_send.at[pushes[0]], row_recv.at[slot, part_of or 0], target))
        pushes[0] += 1

    def got(slot, part_of=None):
        landed(cut_block(slot, part_of), row_recv.at[slot, part_of or 0])

    push(mine, other, 0)
    push(mine, other, 1)
    for d in (2, 1, 3):
        push(mine, x_peers[d - 1])
    push(mine, sibling)
    tables(pairs, table)
    to_scalars = pltpu.make_async_copy(table, steps, load.at[6])
    to_scalars.start()
    prods[96] = jnp.zeros((128, 256), BF16)
    for d in (1, 3, 2):
        slot = zh * 8 + (x + d) % 4 * 2 + k
        got(slot)
        push(slot, sibling)
    for part_of in (0, 1):
        got(far, part_of)
        for d in (2, 1, 3):
            push(far, x_peers[d - 1], part_of)
        push(far, sibling, part_of)
    for part_of in (0, 1):
        for d in (1, 3, 2):
            slot = (1 - zh) * 8 + (x + d) % 4 * 2 + k
            got(slot, part_of)
            push(slot, sibling, part_of)
    for copy in loads[3:]:
        copy.wait()
    to_scalars.wait()
    for n in range(4):
        got(zh * 8 + n * 2 + 1 - k)
        got((1 - zh) * 8 + n * 2 + 1 - k, 0)
        got((1 - zh) * 8 + n * 2 + 1 - k, 1)

    def products(source, base, dims):
        unroll = 32

        def step(i, total):
            for j in range(unroll):
                s = i * unroll + j
                product = dot(tiles[steps[base, s]], source[steps[base + 1, s]], dims)
                total = total * steps[base + 2, s].astype(F32) + product
                prods[s] = total.astype(BF16)
            return total

        lax.fori_loop(0, 96 // unroll, step, jnp.zeros((128, 256), F32))

    def pick(out, b, base):
        out[b] = prods[steps[base + 3, b]]

    products(blocks, 0, ((1,), (0,)))

    near, half = zl % 4, zl // 4
    partner = on_z((zl + 4) % 8)
    edge = near + near // 2 * (3 - 2 * near)
    inward = 1 - 2 * (near // 2)

    def ranked(m):
        both = (2 * edge - m + 4) // 4
        alternate = 1 if m % 2 else -1
        return near + both * alternate * ((m + 1) // 2) + (1 - both) * inward * (m - edge)

    nearest = [ranked(m) for m in (1, 2, 3)]

    place = [nearest[2], nearest[1], nearest[0], near]
    units = [((1 - half) * 4 + n, n, rows, 64) for rows in (0, 64) for n in place]
    units += [(half * 4 + n, n, rows, 64) for rows in (0, 64) for n in place]

    def cut(buffer, index, u):
        return buffer.at[index, pl.ds(units[u][2], units[u][3])]

    def read(buffer, index, u):
        return buffer[index, pl.ds(units[u][2], units[u][3])].astype(F32)

    def sem(group, u):
        return group.at[units[u][0], units[u][2] // 64]

    def turn(u):
        return 1 - 2 * (units[u][1] % 2)

    def send_antipode(u):
        c = units[u][0]
        go(remote(cut(part, block(y + 2, c), u), cut(from_a, c, u), sem(send_a, u), sem(recv_a, u), on_y(turn(u))))

    def send_direct(u):
        c = units[u][0]
        source = cut(part, block(y - turn(u), c), u)
        go(remote(source, cut(from_d, c, u), sem(send_d, u), sem(recv_d, u), on_y(-turn(u))))

    def send_sum(u):
        c, _, rows, count = units[u]
        landed(cut(from_a, c, u), sem(recv_a, u))
        total = read(part, block(y + turn(u), c), u) + read(from_a, c, u)
        staged[c, pl.ds(rows, count)] = total.astype(BF16)
        go(remote(cut(staged, c, u), cut(from_s, c, u), sem(send_s, u), sem(recv_s, u), on_y(turn(u))))

    def sum_y(u):
        c = units[u][0]
        landed(cut(from_d, c, u), sem(recv_d, u))
        landed(cut(from_s, c, u), sem(recv_s, u))
        return read(part, block(y, c), u) + read(from_d, c, u) + read(from_s, c, u)

    def to_place(u):
        c, n, rows, count = units[u]
        summed_y[c, pl.ds(rows, count)] = sum_y(u).astype(BF16)
        slot = u // 8 * 4 + near
        arrival = recv_z.at[slot, rows // 64]
        go(remote(cut(summed_y, c, u), cut(from_z, slot, u), sem(send_z, u), arrival, on_z(half * 4 + n)))

    def sum_half(u):
        total = sum_y(u)
        for d in (1, 2, 3):
            slot = u // 8 * 4 + (near + d) % 4
            landed(cut(from_z, slot, u), recv_z.at[slot, units[u][2] // 64])
            total = total + read(from_z, slot, u)
        return total

    def to_partner(u):
        c, _, rows, count = units[u]
        summed_y[c, pl.ds(rows, count)] = sum_half(u).astype(BF16)
        arrival = recv_z.at[8, rows // 64]
        go(remote(cut(summed_y, c, u), cut(from_z, 8, u), sem(send_z, u), arrival, partner))

    def run(action, *numbers):
        for u in numbers:
            action(u)

    for i in range(4):
        pick(part, block(y + 2, units[i][0]), 0)
        send_antipode(i)
    run(send_antipode, 4, 5, 6, 7)
    for i in range(4):
        pick(part, block(y - turn(i), units[i][0]), 0)
        send_direct(i)
    for i in range(4):
        pick(part, block(y + turn(i), units[i][0]), 0)
        pick(part, block(y, units[i][0]), 0)
    run(send_sum, 0, 1, 2, 3)
    for i in range(8, 12):
        pick(part, block(y + 2, units[i][0]), 0)
        send_antipode(i)
    run(send_direct, 4, 5, 6, 7)
    run(send_sum, 4, 5, 6, 7)
    run(send_antipode, 12, 13, 14, 15)
    for i in range(8, 12):
        for d in (1, 3, 0):
            pick(part, block(y + d, units[i][0]), 0)
    run(send_direct, 8, 9, 10, 11)
    run(to_place, 0, 1, 2)
    run(send_sum, 8, 9, 10, 11)
    run(send_direct, 12, 13, 14, 15)
    run(to_place, 4, 5, 6)
    run(send_sum, 12, 13, 14, 15)
    run(to_partner, 3)
    run(to_place, 8, 9, 10)
    run(to_partner, 7)
    run(to_place, 12, 13, 14)

    here = block(y, zl)

    def activate(n):
        some = pl.ds(n * 64, 64)
        own = sum_half(11 + 4 * n)
        landed(from_z.at[8, some], recv_z.at[8, n])
        own = own + from_z[8, some].astype(F32)
        summed = split_dot(own, weight[...], ((1,), (0,)))
        logistic = 1.0 / (1.0 + jnp.exp(-summed))
        slope = (cotangent[some].astype(F32) * logistic * (1.0 + summed * (1.0 - logistic))).astype(BF16)
        grad[here, some] = slope
        pass_on(here, n, partner)
        to_half(here, n)
        to_sides(here, n)
        activated[some] = (summed * logistic).astype(BF16)
        return split_dot(own, slope, ((0,), (0,)))

    def cut_grad(slot, part_of):
        return grad.at[slot] if part_of is None else grad.at[slot, pl.ds(part_of * 64, 64)]

    def arrived(slot, part_of=None):
        landed(cut_grad(slot, part_of), gather_recv.at[slot, part_of or 0])

    sent = [0]

    def pass_on(slot, part_of, target):
        view = cut_grad(slot, part_of)
        go(remote(view, view, gather_send.at[sent[0]], gather_recv.at[slot, part_of or 0], target))
        sent[0] += 1

    def to_half(slot, part_of):
        for n in nearest:
            pass_on(slot, part_of, on_z(half * 4 + n))

    def to_sides(slot, part_of=None):
        pass_on(slot, part_of, on_y(1))
        pass_on(slot, part_of, on_y(-1))

    def across(c, part_of=None):
        e = 1 - 2 * (c % 2)
        slot = block(y - e, c)
        arrived(slot, part_of)
        pass_on(slot, part_of, on_y(e))

    core_copy = remote(wg.at[pl.ds((1 - k) * 128, 128)], wg_core, wg_send.at[0], wg_recv.at[0], sibling)

    def wg_after_core():
        core_copy.wait_recv()
        wg[pl.ds(pl.multiple_of(k * 128, 128), 128)] += wg_core[...]
        for d in (1, 2, 3):
            rows = pl.ds(pl.multiple_of(k * 128 + (x + d) % 4 * 32, 32), 32)
            go(remote(wg.at[rows], wg_x.at[d], wg_send.at[d], wg_recv.at[d], x_peers[d - 1]))

    def wg_after_x():
        rows = pl.ds(pl.multiple_of(k * 128 + x * 32, 32), 32)
        for d in (1, 2, 3):
            landed(wg_x.at[d], wg_recv.at[d])
        wg_x[0] = wg[rows] + wg_x[1] + wg_x[2] + wg_x[3]
        for d in (1, 2, 3):
            rows = pl.ds(pl.multiple_of((y + d) % 4 * 8, 8), 8)
            go(remote(wg_x.at[0, rows], wg_y.at[d], wg_send.at[3 + d], wg_recv.at[3 + d], y_peers[d - 1]))

    def wg_after_y():
        total = wg_x[0, pl.ds(pl.multiple_of(y * 8, 8), 8)]
        for d in (1, 2, 3):
            landed(wg_y.at[d], wg_recv.at[3 + d])
            total = total + wg_y[d]
        wg_z[z] = total
        for d in range(1, 16):
            go(remote(wg_z.at[z], wg_z.at[z], wg_send.at[6 + d], wg_recv.at[7 + z], z_peers[d - 1]))

    def wg_rows(kk, xx, yy, count):
        return weight_grad.at[pl.ds(pl.multiple_of(kk * 128 + xx * 32 + yy * 8, 8), count)]

    def wg_after_z():
        for d in range(1, 16):
            landed(wg_z.at[(z + d) % 16], wg_recv.at[7 + (z + d) % 16])
        total = wg_z[0]
        for n in range(1, 16):
            total = total + wg_z[n]
        mine_at = wg_rows(k, x, y, 8)
        mine_at[...] = total
        for d in (1, 2, 3):
            go(remote(mine_at, mine_at, back_send.at[d], back_recv.at[y], y_peers[d - 1]))

    def wg_back_x():
        for d in (1, 2, 3):
            landed(wg_rows(k, x, (y + d) % 4, 8), back_recv.at[(y + d) % 4])
        mine_at = wg_rows(k, x, 0, 32)
        for d in (1, 2, 3):
            go(remote(mine_at, mine_at, back_send.at[3 + d], back_recv.at[4 + x], x_peers[d - 1]))

    def wg_back_core():
        for d in (1, 2, 3):
            landed(wg_rows(k, (x + d) % 4, 0, 32), back_recv.at[4 + (x + d) % 4])
        mine_at = wg_rows(k, 0, 0, 128)
        go(remote(mine_at, mine_at, back_send.at[0], back_recv.at[8], sibling))

    def wg_finish():
        landed(wg_rows(1 - k, 0, 0, 128), back_recv.at[8])

    close = [half * 4 + n for n in nearest]
    beyond = (zl + 4) % 8
    distant = [(1 - half) * 4 + n for n in nearest]

    def take(c, part_of=None):
        slot = block(y, c)
        arrived(slot, part_of)
        if c is beyond:
            to_half(slot, part_of)
        to_sides(slot, part_of)

    wg_top = activate(0)
    for c in close:
        take(c, 0)
    across(zl, 0)
    wg[...] = wg_top + activate(1)
    go(core_copy)
    take(beyond, 0)
    for c in close:
        across(c, 0)
    for c in close:
        take(c, 1)
    across(zl, 1)
    wg_after_core()
    for c in distant:
        take(c, 0)
    take(beyond, 1)
    across(beyond, 0)
    for c in close:
        across(c, 1)
    wg_after_x()
    for c in distant:
        across(c, 0)
    for c in distant:
        take(c, 1)
    across(beyond, 1)
    wg_after_y()
    for c in distant:
        across(c, 1)
    for part_of in (0, 1):
        for c in range(8):
            e = 1 - 2 * (c % 2)
            arrived(block(y + e, c), part_of)
            arrived(block(y + 2, c), part_of)

    products(grad, 4, ((0,), (0,)))

    turns = [(h, d) for h in (1 - zh, zh) for d in (2, 1, 3, 0)]
    for h, d in turns:
        slot = h * 4 + (x + d) % 4
        pick(back, slot * 2 + 1 - k, 4)
        go(remote(back.at[slot * 2 + 1 - k], from_core.at[slot], send_core.at[slot], recv_core.at[slot], sibling))
    for h, d in turns:
        pick(back, (h * 4 + (x + d) % 4) * 2 + k, 4)

    def exchanged(h):
        for d in (2, 1, 3, 0):
            slot = h * 4 + (x + d) % 4
            landed(from_core.at[slot], recv_core.at[slot])

    def to_x(h, rows, count):
        some = pl.ds(rows, count)
        for d in (2, 1, 3, 0):
            slot = h * 4 + (x + d) % 4
            total = back[slot * 2 + k, some].astype(F32) + from_core[slot, some].astype(F32)
            if d:
                staged_x[slot, some] = total.astype(BF16)
                go(remote(
                    staged_x.at[slot, some], from_x.at[h * 4 + d, some], send_x.at[slot, rows // 64],
                    recv_x.at[h * 4 + d, rows // 64], x_peers[d - 1]
                ))
            else:
                own_x[h, some] = total

    def sum_x(h, rows, count):
        some = pl.ds(rows, count)
        total = own_x[h, some]
        for d in (1, 3, 2):
            landed(from_x.at[h * 4 + d, some], recv_x.at[h * 4 + d, rows // 64])
            total = total + from_x[h * 4 + d, some].astype(F32)
        return total

    exchanged(1 - zh)
    to_x(1 - zh, 0, 64)
    to_x(1 - zh, 64, 64)
    exchanged(zh)
    to_x(zh, 0, 128)
    wg_after_z()
    for n in (0, 1):
        some = pl.ds(n * 64, 64)
        zh_out[some] = sum_x(1 - zh, n * 64, 64).astype(BF16)
        go(remote(zh_out.at[some], from_zh.at[some], send_zh.at[n], recv_zh.at[n], other))
    wg_back_x()
    backward = sum_x(zh, 0, 128)
    wg_back_core()
    for copy in copies:
        copy.wait_send()
    wg_finish()
    placed = chosen(order[...])
    total = jnp.zeros((128, 256), F32)
    for n in (0, 1):
        landed(from_zh.at[pl.ds(n * 64, 64)], recv_zh.at[n])
        rows = backward[n * 64:n * 64 + 64] + from_zh[n * 64:n * 64 + 64].astype(F32)
        clustered_grad = split_dot(rows, weight[...], ((1,), (1,))).astype(BF16)
        total = total + dot(placed[:, n * 64:n * 64 + 64], clustered_grad, ((1,), (0,)))
    feature_grad[...] = total.astype(BF16)


def body(features, order, weight, tile_values, tile_list, cotangent):
    dma = pltpu.SemaphoreType.DMA

    def slabs(n):
        return pltpu.VMEM((n, 128, 256), BF16)

    operands = (features, order, weight, tile_values[0, 0], tile_list[0, 0].T, cotangent)
    return pl.pallas_call(
        layer_kernel,
        out_shape=(
            jax.ShapeDtypeStruct((128, 256), BF16),
            jax.ShapeDtypeStruct((128, 256), BF16),
            jax.ShapeDtypeStruct((256, 256), F32),
        ),
        in_specs=[pl.BlockSpec(memory_space=pltpu.HBM)] * 6,
        out_specs=(pl.BlockSpec(memory_space=pltpu.VMEM),) * 3,
        scratch_shapes=[
            pltpu.VMEM((128, 256), BF16), pltpu.VMEM((1, 128), jnp.int32), pltpu.VMEM((256, 256), BF16),
            pltpu.VMEM((96, 128, 128), BF16), pltpu.VMEM((2, 96), jnp.int32), pltpu.VMEM((128, 256), BF16),
            pltpu.VMEM((8, 128), jnp.int32), pltpu.SMEM((8, 128), jnp.int32), dma((7,)),
            slabs(16), slabs(97), slabs(32), slabs(32), slabs(16),
            slabs(8), slabs(8), slabs(8), slabs(8), slabs(8), slabs(9),
            pltpu.VMEM((256, 256), F32), pltpu.VMEM((128, 256), F32), pltpu.VMEM((4, 32, 256), F32),
            pltpu.VMEM((4, 8, 256), F32), pltpu.VMEM((16, 8, 256), F32),
            slabs(8), slabs(8), slabs(8), pltpu.VMEM((2, 128, 256), F32),
            pltpu.VMEM((128, 256), BF16), pltpu.VMEM((128, 256), BF16),
            dma((23,)), dma((16, 2)),
            dma((8, 2)), dma((8, 2)), dma((8, 2)), dma((8, 2)), dma((8, 2)), dma((8, 2)), dma((8, 2)), dma((9, 2)),
            dma((62,)), dma((32, 2)), dma((22,)), dma((23,)),
            dma((8,)), dma((8,)), dma((8, 2)), dma((8, 2)), dma((2,)), dma((2,)), dma((7,)), dma((9,)),
        ],
        compiler_params=pltpu.CompilerParams(collective_id=0, has_side_effects=True, vmem_limit_bytes=VMEM_LIMIT),
        name="layer",
    )(*[pltpu.with_memory_space_constraint(operand, pltpu.HBM) for operand in operands])


def solution(mesh):
    placed = (
        P(("row", "col"), None),
        P(("row", "col"), None),
        P(),
        P("row", "col", None, None, None),
        P("row", "col", None, None),
        P(("row", "col"), None),
    )
    return jax.shard_map(
        body,
        mesh=mesh,
        in_specs=placed,
        out_specs=(P(("row", "col"), None), P(("row", "col"), None), P()),
        check_vma=False,
    )
```

```python
import jax
import jax.numpy as jnp
from jax import lax
from jax.experimental import pallas as pl
from jax.experimental.pallas import tpu as pltpu
from jax.sharding import PartitionSpec as P

MESH = pl.DeviceIdType.MESH
F32 = jnp.float32
BF16 = jnp.bfloat16
VMEM_LIMIT = 52 << 20


def position():
    row, col = lax.axis_index("row"), lax.axis_index("col")
    return row // 8, row // 2 % 4, row % 2, col // 8, col % 8


def device(zh, x, k, y, zl):
    return {"row": zh * 8 + x * 2 + k, "col": y * 8 + zl}


def remote(src, dst, send, recv, target):
    return pltpu.make_async_remote_copy(
        src_ref=src, dst_ref=dst, send_sem=send, recv_sem=recv, device_id=target, device_id_type=MESH
    )


def dot(a, b, dims):
    return lax.dot_general(a, b, (dims, ((), ())), preferred_element_type=F32)


def split_dot(a, b, dims):
    high = a.astype(BF16)
    low = (a - high.astype(F32)).astype(BF16)
    return dot(high, b, dims) + dot(low, b, dims)


def chosen(order):
    rows = lax.broadcasted_iota(jnp.int32, (128, 128), 0)
    return jnp.where(rows == order, 1.0, 0.0).astype(BF16)


def tables(pairs, table):
    n = pairs.shape[1]
    down = lax.broadcasted_iota(jnp.int32, (n, n), 0)
    across = lax.broadcasted_iota(jnp.int32, (n, n), 1)
    same = down == across

    def column(row):
        return jnp.sum(jnp.where(same, row, 0), axis=1, keepdims=True)

    p_row, q_row = pairs[0:1, :], pairs[1:2, :]
    lane = lax.broadcasted_iota(jnp.int32, (1, n), 1)
    for base, major_row, minor_row in ((0, p_row, q_row), (4, q_row, p_row)):
        key_row = jnp.where(p_row >= 0, major_row * 32 + minor_row, 2048 + lane)
        key, major, minor = column(key_row), column(major_row), column(minor_row)
        before = key_row < key
        rank = jnp.sum(jnp.where(before, 1, 0), axis=1, keepdims=True)
        goes_on = jnp.sum(jnp.where(before & (major_row == major), 1, 0), axis=1, keepdims=True)
        hit = rank == across

        def sort(values, most):
            return jnp.minimum(jnp.sum(jnp.where(hit, values, 0), axis=0, keepdims=True), most)

        table[base:base + 1, 0:n] = sort(down, n - 1)
        table[base + 1:base + 2, 0:n] = sort(jnp.maximum(minor, 0), 31 if base else 15)
        table[base + 2:base + 3, 0:n] = sort(jnp.minimum(goes_on, 1), 1)
        upto = jnp.sum(jnp.where((major >= 0) & (major <= across), 1, 0), axis=0, keepdims=True)
        here = jnp.sum(jnp.where(major == across, 1, 0), axis=0, keepdims=True)
        table[base + 3:base + 4, 0:n] = jnp.where(here > 0, upto - 1, n)


def layer_kernel(
    features_hbm, order_hbm, weight_hbm, tiles_hbm, pairs_hbm, cotangent_hbm,
    activated, feature_grad, weight_grad,
    features, order, weight, tiles, pairs, cotangent, table, steps, load,
    blocks, prods, part, grad, back,
    from_a, from_d, from_s, staged, summed_y, from_z,
    wg, wg_core, wg_x, wg_y, wg_z,
    from_core, staged_x, from_x, own_x, zh_out, from_zh,
    row_send, row_recv,
    send_a, send_d, send_s, send_z, recv_a, recv_d, recv_s, recv_z,
    gather_send, gather_recv, wg_send, wg_recv,
    send_core, recv_core, send_x, recv_x, send_zh, recv_zh, back_send, back_recv,
):
    zh, x, k, y, zl = position()

    def on_y(d):
        return device(zh, x, k, (y + d + 4) % 4, zl)

    def on_z(z):
        return device(zh, x, k, y, z)

    def block(yy, c):
        return (yy + 4) % 4 * 8 + c

    sibling = device(zh, x, 1 - k, y, zl)
    other = device(1 - zh, x, k, y, zl)
    x_peers = [device(zh, (x + d) % 4, k, y, zl) for d in (1, 2, 3)]
    y_peers = [on_y(d) for d in (1, 2, 3)]
    z = zh * 8 + zl
    z_peers = [device((z + d) % 16 // 8, x, k, y, (z + d) % 8) for d in range(1, 16)]
    everyone = [z_peers[8 + d - 1] for d in (0, -1, 1, -2, 2, -3, 3, -4, 4, -5, 5, -6, 6, -7, 7)] + x_peers + y_peers + [sibling]
    barrier = pltpu.get_barrier_semaphore()
    for target in everyone:
        pl.semaphore_signal(barrier, inc=1, device_id=target, device_id_type=MESH)

    loads = [
        pltpu.make_async_copy(hbm, vmem, load.at[n])
        for n, (hbm, vmem) in enumerate((
            (features_hbm, features), (order_hbm, order), (pairs_hbm, pairs),
            (weight_hbm, weight), (cotangent_hbm, cotangent), (tiles_hbm, tiles),
        ))
    ]
    for copy in loads:
        copy.start()
    copies = []

    def go(copy):
        copy.start()
        copies.append(copy)

    def landed(buffer, sem):
        remote(buffer, buffer, sem, sem, sibling).wait_recv()

    mine = zh * 8 + x * 2 + k
    far = (1 - zh) * 8 + x * 2 + k
    loads[0].wait()
    loads[1].wait()
    blocks[mine] = dot(chosen(order[...]), features[...], ((0,), (0,))).astype(BF16)
    loads[2].wait()
    pl.semaphore_wait(barrier, len(everyone))
    pushes = [0]

    def cut_block(slot, part_of):
        return blocks.at[slot] if part_of is None else blocks.at[slot, pl.ds(part_of * 64, 64)]

    def push(slot, target, part_of=None):
        view = cut_block(slot, part_of)
        go(remote(view, view, row_send.at[pushes[0]], row_recv.at[slot, part_of or 0], target))
        pushes[0] += 1

    def got(slot, part_of=None):
        landed(cut_block(slot, part_of), row_recv.at[slot, part_of or 0])

    push(mine, other, 0)
    push(mine, other, 1)
    for d in (2, 1, 3):
        push(mine, x_peers[d - 1])
    push(mine, sibling)
    tables(pairs, table)
    to_scalars = pltpu.make_async_copy(table, steps, load.at[6])
    to_scalars.start()
    prods[96] = jnp.zeros((128, 256), BF16)
    for d in (1, 3, 2):
        slot = zh * 8 + (x + d) % 4 * 2 + k
        got(slot)
        push(slot, sibling)
    for part_of in (0, 1):
        got(far, part_of)
        for d in (2, 1, 3):
            push(far, x_peers[d - 1], part_of)
        push(far, sibling, part_of)
    for part_of in (0, 1):
        for d in (1, 3, 2):
            slot = (1 - zh) * 8 + (x + d) % 4 * 2 + k
            got(slot, part_of)
            push(slot, sibling, part_of)
    for copy in loads[3:]:
        copy.wait()
    to_scalars.wait()
    for n in range(4):
        got(zh * 8 + n * 2 + 1 - k)
        got((1 - zh) * 8 + n * 2 + 1 - k, 0)
        got((1 - zh) * 8 + n * 2 + 1 - k, 1)

    def products(source, base, dims):
        unroll = 32

        def step(i, total):
            for j in range(unroll):
                s = i * unroll + j
                product = dot(tiles[steps[base, s]], source[steps[base + 1, s]], dims)
                total = total * steps[base + 2, s].astype(F32) + product
                prods[s] = total.astype(BF16)
            return total

        lax.fori_loop(0, 96 // unroll, step, jnp.zeros((128, 256), F32))

    def pick(out, b, base):
        out[b] = prods[steps[base + 3, b]]

    products(blocks, 0, ((1,), (0,)))

    near, half = zl % 4, zl // 4
    partner = on_z((zl + 4) % 8)
    edge = near + near // 2 * (3 - 2 * near)
    inward = 1 - 2 * (near // 2)

    def ranked(m):
        both = (2 * edge - m + 4) // 4
        alternate = 1 if m % 2 else -1
        return near + both * alternate * ((m + 1) // 2) + (1 - both) * inward * (m - edge)

    nearest = [ranked(m) for m in (1, 2, 3)]

    place = [nearest[2], nearest[1], nearest[0], near]
    units = [((1 - half) * 4 + n, n, rows, 64) for rows in (0, 64) for n in place]
    units += [(half * 4 + n, n, rows, 64) for rows in (0, 64) for n in place]

    def cut(buffer, index, u):
        return buffer.at[index, pl.ds(units[u][2], units[u][3])]

    def read(buffer, index, u):
        return buffer[index, pl.ds(units[u][2], units[u][3])].astype(F32)

    def sem(group, u):
        return group.at[units[u][0], units[u][2] // 64]

    def turn(u):
        return 1 - 2 * (units[u][1] % 2)

    def send_antipode(u):
        c = units[u][0]
        go(remote(cut(part, block(y + 2, c), u), cut(from_a, c, u), sem(send_a, u), sem(recv_a, u), on_y(turn(u))))

    def send_direct(u):
        c = units[u][0]
        source = cut(part, block(y - turn(u), c), u)
        go(remote(source, cut(from_d, c, u), sem(send_d, u), sem(recv_d, u), on_y(-turn(u))))

    def send_sum(u):
        c, _, rows, count = units[u]
        landed(cut(from_a, c, u), sem(recv_a, u))
        total = read(part, block(y + turn(u), c), u) + read(from_a, c, u)
        staged[c, pl.ds(rows, count)] = total.astype(BF16)
        go(remote(cut(staged, c, u), cut(from_s, c, u), sem(send_s, u), sem(recv_s, u), on_y(turn(u))))

    def sum_y(u):
        c = units[u][0]
        landed(cut(from_d, c, u), sem(recv_d, u))
        landed(cut(from_s, c, u), sem(recv_s, u))
        return read(part, block(y, c), u) + read(from_d, c, u) + read(from_s, c, u)

    def to_place(u):
        c, n, rows, count = units[u]
        summed_y[c, pl.ds(rows, count)] = sum_y(u).astype(BF16)
        slot = u // 8 * 4 + near
        arrival = recv_z.at[slot, rows // 64]
        go(remote(cut(summed_y, c, u), cut(from_z, slot, u), sem(send_z, u), arrival, on_z(half * 4 + n)))

    def sum_half(u):
        total = sum_y(u)
        for d in (1, 2, 3):
            slot = u // 8 * 4 + (near + d) % 4
            landed(cut(from_z, slot, u), recv_z.at[slot, units[u][2] // 64])
            total = total + read(from_z, slot, u)
        return total

    def to_partner(u):
        c, _, rows, count = units[u]
        summed_y[c, pl.ds(rows, count)] = sum_half(u).astype(BF16)
        arrival = recv_z.at[8, rows // 64]
        go(remote(cut(summed_y, c, u), cut(from_z, 8, u), sem(send_z, u), arrival, partner))

    def run(action, *numbers):
        for u in numbers:
            action(u)

    for i in range(4):
        pick(part, block(y + 2, units[i][0]), 0)
        send_antipode(i)
    run(send_antipode, 4, 5, 6, 7)
    for i in range(4):
        pick(part, block(y - turn(i), units[i][0]), 0)
        send_direct(i)
    for i in range(4):
        pick(part, block(y + turn(i), units[i][0]), 0)
        pick(part, block(y, units[i][0]), 0)
    run(send_sum, 0, 1, 2, 3)
    for i in range(8, 12):
        pick(part, block(y + 2, units[i][0]), 0)
        send_antipode(i)
    run(send_direct, 4, 5, 6, 7)
    run(send_sum, 4, 5, 6, 7)
    run(send_antipode, 12, 13, 14, 15)
    for i in range(8, 12):
        for d in (1, 3, 0):
            pick(part, block(y + d, units[i][0]), 0)
    run(send_direct, 8, 9, 10, 11)
    run(to_place, 0, 1, 2)
    run(send_sum, 8, 9, 10, 11)
    run(send_direct, 12, 13, 14, 15)
    run(to_place, 4, 5, 6)
    run(send_sum, 12, 13, 14, 15)
    run(to_partner, 3)
    run(to_place, 8, 9, 10)
    run(to_partner, 7)
    run(to_place, 12, 13, 14)

    here = block(y, zl)

    def activate(n):
        some = pl.ds(n * 64, 64)
        own = sum_half(11 + 4 * n)
        landed(from_z.at[8, some], recv_z.at[8, n])
        own = own + from_z[8, some].astype(F32)
        summed = split_dot(own, weight[...], ((1,), (0,)))
        logistic = 1.0 / (1.0 + jnp.exp(-summed))
        slope = (cotangent[some].astype(F32) * logistic * (1.0 + summed * (1.0 - logistic))).astype(BF16)
        grad[here, some] = slope
        pass_on(here, n, partner)
        to_half(here, n)
        to_sides(here, n)
        activated[some] = (summed * logistic).astype(BF16)
        return split_dot(own, slope, ((0,), (0,)))

    def cut_grad(slot, part_of):
        return grad.at[slot] if part_of is None else grad.at[slot, pl.ds(part_of * 64, 64)]

    def arrived(slot, part_of=None):
        landed(cut_grad(slot, part_of), gather_recv.at[slot, part_of or 0])

    sent = [0]

    def pass_on(slot, part_of, target):
        view = cut_grad(slot, part_of)
        go(remote(view, view, gather_send.at[sent[0]], gather_recv.at[slot, part_of or 0], target))
        sent[0] += 1

    def to_half(slot, part_of):
        for n in nearest:
            pass_on(slot, part_of, on_z(half * 4 + n))

    def to_sides(slot, part_of=None):
        pass_on(slot, part_of, on_y(1))
        pass_on(slot, part_of, on_y(-1))

    def across(c, part_of=None):
        e = 1 - 2 * (c % 2)
        slot = block(y - e, c)
        arrived(slot, part_of)
        pass_on(slot, part_of, on_y(e))

    core_copy = remote(wg.at[pl.ds((1 - k) * 128, 128)], wg_core, wg_send.at[0], wg_recv.at[0], sibling)

    def wg_after_core():
        core_copy.wait_recv()
        wg[pl.ds(pl.multiple_of(k * 128, 128), 128)] += wg_core[...]
        for d in (1, 2, 3):
            rows = pl.ds(pl.multiple_of(k * 128 + (x + d) % 4 * 32, 32), 32)
            go(remote(wg.at[rows], wg_x.at[d], wg_send.at[d], wg_recv.at[d], x_peers[d - 1]))

    def wg_after_x():
        rows = pl.ds(pl.multiple_of(k * 128 + x * 32, 32), 32)
        for d in (1, 2, 3):
            landed(wg_x.at[d], wg_recv.at[d])
        wg_x[0] = wg[rows] + wg_x[1] + wg_x[2] + wg_x[3]
        for d in (1, 2, 3):
            rows = pl.ds(pl.multiple_of((y + d) % 4 * 8, 8), 8)
            go(remote(wg_x.at[0, rows], wg_y.at[d], wg_send.at[3 + d], wg_recv.at[3 + d], y_peers[d - 1]))

    def wg_after_y():
        total = wg_x[0, pl.ds(pl.multiple_of(y * 8, 8), 8)]
        for d in (1, 2, 3):
            landed(wg_y.at[d], wg_recv.at[3 + d])
            total = total + wg_y[d]
        wg_z[z] = total
        for d in range(1, 16):
            go(remote(wg_z.at[z], wg_z.at[z], wg_send.at[6 + d], wg_recv.at[7 + z], z_peers[d - 1]))

    def wg_rows(kk, xx, yy, count):
        return weight_grad.at[pl.ds(pl.multiple_of(kk * 128 + xx * 32 + yy * 8, 8), count)]

    def wg_after_z():
        for d in range(1, 16):
            landed(wg_z.at[(z + d) % 16], wg_recv.at[7 + (z + d) % 16])
        total = wg_z[0]
        for n in range(1, 16):
            total = total + wg_z[n]
        mine_at = wg_rows(k, x, y, 8)
        mine_at[...] = total
        for d in (1, 2, 3):
            go(remote(mine_at, mine_at, back_send.at[d], back_recv.at[y], y_peers[d - 1]))

    def wg_back_x():
        for d in (1, 2, 3):
            landed(wg_rows(k, x, (y + d) % 4, 8), back_recv.at[(y + d) % 4])
        mine_at = wg_rows(k, x, 0, 32)
        for d in (1, 2, 3):
            go(remote(mine_at, mine_at, back_send.at[3 + d], back_recv.at[4 + x], x_peers[d - 1]))

    def wg_back_core():
        for d in (1, 2, 3):
            landed(wg_rows(k, (x + d) % 4, 0, 32), back_recv.at[4 + (x + d) % 4])
        mine_at = wg_rows(k, 0, 0, 128)
        go(remote(mine_at, mine_at, back_send.at[0], back_recv.at[8], sibling))

    def wg_finish():
        landed(wg_rows(1 - k, 0, 0, 128), back_recv.at[8])

    close = [half * 4 + n for n in nearest]
    beyond = (zl + 4) % 8
    distant = [(1 - half) * 4 + n for n in nearest]

    def take(c, part_of=None):
        slot = block(y, c)
        arrived(slot, part_of)
        if c is beyond:
            to_half(slot, part_of)
        to_sides(slot, part_of)

    wg_top = activate(0)
    for c in close:
        take(c, 0)
    across(zl, 0)
    wg[...] = wg_top + activate(1)
    go(core_copy)
    take(beyond, 0)
    for c in close:
        across(c, 0)
    for c in close:
        take(c, 1)
    across(zl, 1)
    wg_after_core()
    for c in distant:
        take(c, 0)
    take(beyond, 1)
    across(beyond, 0)
    for c in close:
        across(c, 1)
    wg_after_x()
    for c in distant:
        across(c, 0)
    for c in distant:
        take(c, 1)
    across(beyond, 1)
    wg_after_y()
    for c in distant:
        across(c, 1)
    for part_of in (0, 1):
        for c in range(8):
            e = 1 - 2 * (c % 2)
            arrived(block(y + e, c), part_of)
            arrived(block(y + 2, c), part_of)

    products(grad, 4, ((0,), (0,)))

    turns = [(h, d) for h in (1 - zh, zh) for d in (2, 1, 3, 0)]
    for h, d in turns:
        slot = h * 4 + (x + d) % 4
        pick(back, slot * 2 + 1 - k, 4)
        go(remote(back.at[slot * 2 + 1 - k], from_core.at[slot], send_core.at[slot], recv_core.at[slot], sibling))
    for h, d in turns:
        pick(back, (h * 4 + (x + d) % 4) * 2 + k, 4)

    def exchanged(h):
        for d in (2, 1, 3, 0):
            slot = h * 4 + (x + d) % 4
            landed(from_core.at[slot], recv_core.at[slot])

    def to_x(h, rows, count):
        some = pl.ds(rows, count)
        for d in (2, 1, 3, 0):
            slot = h * 4 + (x + d) % 4
            total = back[slot * 2 + k, some].astype(F32) + from_core[slot, some].astype(F32)
            if d:
                staged_x[slot, some] = total.astype(BF16)
                go(remote(
                    staged_x.at[slot, some], from_x.at[h * 4 + d, some], send_x.at[slot, rows // 64],
                    recv_x.at[h * 4 + d, rows // 64], x_peers[d - 1]
                ))
            else:
                own_x[h, some] = total

    def sum_x(h, rows, count):
        some = pl.ds(rows, count)
        total = own_x[h, some]
        for d in (1, 3, 2):
            landed(from_x.at[h * 4 + d, some], recv_x.at[h * 4 + d, rows // 64])
            total = total + from_x[h * 4 + d, some].astype(F32)
        return total

    exchanged(1 - zh)
    to_x(1 - zh, 0, 64)
    to_x(1 - zh, 64, 64)
    exchanged(zh)
    to_x(zh, 0, 128)
    wg_after_z()
    for n in (0, 1):
        some = pl.ds(n * 64, 64)
        zh_out[some] = sum_x(1 - zh, n * 64, 64).astype(BF16)
        go(remote(zh_out.at[some], from_zh.at[some], send_zh.at[n], recv_zh.at[n], other))
    wg_back_x()
    backward = sum_x(zh, 0, 128)
    wg_back_core()
    for copy in copies:
        copy.wait_send()
    wg_finish()
    placed = chosen(order[...])
    total = jnp.zeros((128, 256), F32)
    for n in (0, 1):
        landed(from_zh.at[pl.ds(n * 64, 64)], recv_zh.at[n])
        rows = backward[n * 64:n * 64 + 64] + from_zh[n * 64:n * 64 + 64].astype(F32)
        clustered_grad = split_dot(rows, weight[...], ((1,), (1,))).astype(BF16)
        total = total + dot(placed[:, n * 64:n * 64 + 64], clustered_grad, ((1,), (0,)))
    feature_grad[...] = total.astype(BF16)


def body(features, order, weight, tile_values, tile_list, cotangent):
    dma = pltpu.SemaphoreType.DMA

    def slabs(n):
        return pltpu.VMEM((n, 128, 256), BF16)

    operands = (features, order, weight, tile_values[0, 0], tile_list[0, 0].T, cotangent)
    return pl.pallas_call(
        layer_kernel,
        out_shape=(
            jax.ShapeDtypeStruct((128, 256), BF16),
            jax.ShapeDtypeStruct((128, 256), BF16),
            jax.ShapeDtypeStruct((256, 256), F32),
        ),
        in_specs=[pl.BlockSpec(memory_space=pltpu.HBM)] * 6,
        out_specs=(pl.BlockSpec(memory_space=pltpu.VMEM),) * 3,
        scratch_shapes=[
            pltpu.VMEM((128, 256), BF16), pltpu.VMEM((1, 128), jnp.int32), pltpu.VMEM((256, 256), BF16),
            pltpu.VMEM((96, 128, 128), BF16), pltpu.VMEM((2, 96), jnp.int32), pltpu.VMEM((128, 256), BF16),
            pltpu.VMEM((8, 128), jnp.int32), pltpu.SMEM((8, 128), jnp.int32), dma((7,)),
            slabs(16), slabs(97), slabs(32), slabs(32), slabs(16),
            slabs(8), slabs(8), slabs(8), slabs(8), slabs(8), slabs(9),
            pltpu.VMEM((256, 256), F32), pltpu.VMEM((128, 256), F32), pltpu.VMEM((4, 32, 256), F32),
            pltpu.VMEM((4, 8, 256), F32), pltpu.VMEM((16, 8, 256), F32),
            slabs(8), slabs(8), slabs(8), pltpu.VMEM((2, 128, 256), F32),
            pltpu.VMEM((128, 256), BF16), pltpu.VMEM((128, 256), BF16),
            dma((23,)), dma((16, 2)),
            dma((8, 2)), dma((8, 2)), dma((8, 2)), dma((8, 2)), dma((8, 2)), dma((8, 2)), dma((8, 2)), dma((9, 2)),
            dma((62,)), dma((32, 2)), dma((22,)), dma((23,)),
            dma((8,)), dma((8,)), dma((8, 2)), dma((8, 2)), dma((2,)), dma((2,)), dma((7,)), dma((9,)),
        ],
        compiler_params=pltpu.CompilerParams(collective_id=0, has_side_effects=True, vmem_limit_bytes=VMEM_LIMIT),
        name="layer",
    )(*[pltpu.with_memory_space_constraint(operand, pltpu.HBM) for operand in operands])


def solution(mesh):
    placed = (
        P(("row", "col"), None),
        P(("row", "col"), None),
        P(),
        P("row", "col", None, None, None),
        P("row", "col", None, None),
        P(("row", "col"), None),
    )
    return jax.shard_map(
        body,
        mesh=mesh,
        in_specs=placed,
        out_specs=(P(("row", "col"), None), P(("row", "col"), None), P()),
        check_vma=False,
    )
```
